32 devices in a mesh: groups: 2 (over x), expert: 16 (over z, y, core), tensor: 1.
Axes of the slice: x: 2, y: 2, z: 4, core: 2. Of those that a mesh axis runs over, the one named last changes fastest.
Arguments:
- queries: bfloat16 [2048, 64, 288], P(('groups', 'expert'), 'tensor'), parts along dimension 0, may hold values from -64 to 64
- kv_latent: bfloat16 [2048, 288], P(('groups', 'expert')), parts along dimension 0, may hold values from -5 to 5
- value_up: bfloat16 [64, 256, 128], P('tensor', 'expert'), may hold values from -0.375 to 0.375
- out_proj: bfloat16 [8192, 3584], P('tensor', 'expert'), may hold values from -0.0625 to 0.0625
- norm_gain: float32 [3584], replicated, may hold values from 0.25 to 1.75
- gate_proj: bfloat16 [16, 3584, 1024], P('expert', None, 'tensor'), may hold values from -0.09375 to 0.09375
- up_proj: bfloat16 [16, 3584, 1024], P('expert', None, 'tensor'), may hold values from -0.09375 to 0.09375
- down_proj: bfloat16 [16, 1024, 3584], P('expert', 'tensor'), may hold values from -0.1875 to 0.1875
- routes: int32 [2048, 8], P(('groups', 'expert', 'tensor')), parts along dimension 0, may hold values from 0 to 15, all different within a row; in each aligned block of 64 rows (0 to 63, 64 to 127, ...) at most 40 rows name the same one
- route_weights: float32 [2048, 8], P(('groups', 'expert', 'tensor')), parts along dimension 0, may hold values from 0.05 to 0.6
Outputs:
- layer_out: bfloat16 [2048, 3584], P(('groups', 'expert', 'tensor')), parts along dimension 0
The draws below stay inside these ranges and needn't reach their ends.
There are 2 independent parts, one for each index of `groups`. The reference program is written for one: setup_inputs(seed, part) draws one part's arguments, and reference() takes and returns one part's arrays. A program takes and returns all parts, laid end to end along the dimension named above; an argument that names none is the same for every part. Nothing has to cross between parts.
Inputs may be any that keep to these rules, and one draw needn't show every extreme that they name: `routes`: the tokens of one device (aligned blocks of 64 rows) name no expert more than 40 times; each token names 8 different experts.
All inputs are finite; a program needn't handle non-finite values.
Results may differ from the reference program's by a relative error of at most 0.029.
Values may be sent and summed in bfloat16 or wider, within the bound.
No kernel may reach another device: no remote copies, remote signals or barrier semaphores. Data moves between devices by JAX's collectives and lax.ppermute only.
A program may use at most 128 MiB of HBM per device.

```python
import math
import jax
import jax.numpy as jnp
import numpy as np
from jax import lax

D = 3584
H = 64
LAT = 256
ROPE = 32
VD = 128
FF = 1024
TOP = 8
SEQ = 1024
ROWS = 64
EXPERTS = 16
CAP = 40


def shared_keys(key):
    return jnp.clip(jax.random.normal(key, (SEQ, LAT + ROPE), jnp.float32), -5.0, 5.0)


def draw_kv_latent(key, part):
    return shared_keys(key).astype(jnp.bfloat16)


def draw_queries(key, part):
    key = jax.random.fold_in(key, 5)
    noise = jax.random.normal(key, (SEQ, H, LAT + ROPE), jnp.float32)
    return jnp.clip(noise, -64.0, 64.0).astype(jnp.bfloat16)


def steps_of(rng, shape, split, least, high):
    level, own = 1.0, jax.random.fold_in(rng, 6)
    for axis_at, parts in split:
        steps = jnp.exp(jax.random.uniform(jax.random.fold_in(own, axis_at), (parts,), jnp.float32, least / len(split), high / len(split)))
        level = level * jnp.repeat(steps, shape[axis_at] // parts).reshape([-1 if axis == axis_at else 1 for axis in range(len(shape))])
    return level


def deal_out(key, own, number, rows, amount, top, reach, slope):
    order = jax.random.permutation(key, amount)
    crowded, usual = portions_of(amount, rows * top, reach, slope, True), portions_of(amount, rows * top, reach, slope, False)
    places = jnp.arange(amount)

    def named(tallies, turn):
        used = int((tallies > 0).sum())
        fixed = max(1, used // 4)
        shifted = fixed + (places - fixed + turn * (used - fixed)) % max(1, amount - fixed)
        return jnp.zeros((amount,), jnp.int32).at[order[jnp.where(places < fixed, places, shifted)]].set(jnp.asarray(tallies, jnp.int32))

    tallies = jnp.where(number % 4 == 0, named(crowded, number // 4), named(usual, number - number // 4 - 1))
    mixed = jax.random.permutation(jax.random.fold_in(own, 3), amount)
    donor, taker = mixed[0:amount // 2 * 2:2], mixed[1:amount // 2 * 2:2]
    margin = jnp.minimum(tallies[donor] - 1, reach - tallies[taker]) // 2
    margin = jnp.where((donor == order[0]) | (taker == order[0]) | (tallies[taker] == 0), 0, jnp.maximum(margin, 0))
    shifted = jax.random.randint(jax.random.fold_in(own, 4), (amount // 2,), 0, 1 << 20) % (margin + 1)
    tallies = tallies.at[donor].add(-shifted).at[taker].add(shifted)
    labels = jnp.searchsorted(jnp.cumsum(tallies), jnp.arange(rows * top), side="right").astype(jnp.int32)
    grid = labels.reshape(top, rows).T
    grid = grid[jax.random.permutation(jax.random.fold_in(own, 1), rows)]
    turn = jax.random.randint(jax.random.fold_in(own, 2), (rows, 1), 0, top)
    return jnp.take_along_axis(grid, (jnp.arange(top)[None, :] + turn) % top, axis=1)


def portions_of(count, total, reach, lean, full):
    portions = [(1 << 20) // math.isqrt(grade ** lean) + 1 for grade in range(1, count + 1)]
    largest = reach if full else min(reach, max(-(-total // count), total * portions[0] // sum(portions)))
    least = 1 if total - largest >= count - 1 else 0
    holding, rest = [largest] + [least] * (count - 1), total - largest - least * (count - 1)
    while rest > 0:
        movable = [i for i in range(1, count) if holding[i] < largest] or [i for i in range(1, count) if holding[i] < reach]
        pool, budget = sum([portions[i] for i in movable]), rest
        for i in movable:
            more = min(reach - holding[i], max(1, budget * portions[i] // pool), rest)
            holding[i] = holding[i] + more
            rest = rest - more
    return np.array(holding)


def bell_draw(own_key, dims, spread, reach, pieces=(), kind=jnp.bfloat16):
    result = spread * jax.random.normal(own_key, dims, jnp.float32)
    if pieces:
        result = result * steps_of(own_key, dims, pieces, -0.22, 0.18)
    return jnp.clip(result, -reach, reach).astype(kind)


def setup_inputs(seed: int = 0, part: int = 0) -> dict:
    streams_of = jax.random.split(jax.random.key(seed), 11)
    own_keys = jax.random.split(jax.random.fold_in(streams_of[10], part), 11)
    queries = draw_queries(jax.random.fold_in(jax.random.fold_in(streams_of[10], part), 71), part)
    kv_latent = draw_kv_latent(jax.random.fold_in(jax.random.fold_in(streams_of[10], part), 71), part)
    value_up = bell_draw(streams_of[2], (H, LAT, VD), LAT ** -0.5, 0.375, ((1, 16),))
    out_proj = bell_draw(streams_of[3], (H * VD, D), (H * VD) ** -0.5, 0.0625, ((1, 16),))
    norm_gain = jnp.clip(1.0 + 0.15 * jax.random.normal(streams_of[4], (D,), jnp.float32), 0.25, 1.75)
    gate_proj = bell_draw(streams_of[5], (EXPERTS, D, FF), D ** -0.5, 0.09375, ((0, 16),))
    up_proj = bell_draw(streams_of[6], (EXPERTS, D, FF), D ** -0.5, 0.09375, ((0, 16),))
    down_proj = bell_draw(streams_of[7], (EXPERTS, FF, D), FF ** -0.5, 0.1875, ((0, 16),))
    routes_keys = jax.random.split(jax.random.fold_in(own_keys[8], 1), SEQ // ROWS)
    routes_turns = jax.random.permutation(jax.random.fold_in(own_keys[8], 3), SEQ // ROWS)
    routes = jax.vmap(lambda own, number: deal_out(jax.random.fold_in(own_keys[8], 2), own, number, ROWS, EXPERTS, TOP, CAP, 2))(routes_keys, routes_turns).reshape((SEQ, TOP))
    route_weights = jnp.clip(0.05 + 0.55 * jax.random.uniform(own_keys[9], (SEQ, TOP), jnp.float32) ** steps_of(own_keys[9], (SEQ, TOP), ((0, 16),), -0.2, 0.2), 0.05, 0.6)
    return {"queries": queries, "kv_latent": kv_latent, "value_up": value_up, "out_proj": out_proj, "norm_gain": norm_gain, "gate_proj": gate_proj, "up_proj": up_proj, "down_proj": down_proj, "routes": routes, "route_weights": route_weights}


score_scale = 0.0722

def reference(queries, kv_latent, value_up, out_proj, norm_gain, gate_proj, up_proj, down_proj, routes, route_weights):
    places = jnp.arange(SEQ)
    allowed = places[:, None] >= places[None, :]
    values = kv_latent[:, :LAT]

    def one_head(q_head):
        scores = jnp.dot(q_head, kv_latent.T, preferred_element_type=jnp.float32) * score_scale
        scores = jnp.where(allowed, scores, -1e+30)
        top = lax.optimization_barrier(jnp.max(scores, axis=-1, keepdims=True))
        expo = jnp.where(allowed, jnp.exp(scores - top), 0.0)
        total = lax.optimization_barrier(jnp.sum(expo, axis=-1, keepdims=True))
        weights = expo.astype(jnp.bfloat16)
        return jnp.dot(weights, values, preferred_element_type=jnp.float32) / total
    latent_out = lax.map(one_head, jnp.transpose(queries, (1, 0, 2)))
    latent_out = jnp.transpose(latent_out, (1, 0, 2)).astype(jnp.bfloat16)
    heads_out = jnp.einsum('shc,hcv->shv', latent_out.astype(jnp.float32), value_up.astype(jnp.float32)).astype(jnp.bfloat16)
    attn = jnp.dot(heads_out.reshape(SEQ, H * VD), out_proj, preferred_element_type=jnp.float32)
    attn_out = attn.astype(jnp.bfloat16)
    attn32 = attn_out.astype(jnp.float32)
    scale = lax.rsqrt(lax.optimization_barrier(jnp.mean(attn32 * attn32, axis=-1, keepdims=True)) + 1e-06)
    normed = (attn32 * scale * norm_gain).astype(jnp.bfloat16)

    def one_expert(mats):
        gate_w, up_w, down_w = mats
        gate = jnp.dot(normed, gate_w, preferred_element_type=jnp.float32)
        upper = jnp.dot(normed, up_w, preferred_element_type=jnp.float32)
        hidden = (jax.nn.silu(gate) * upper).astype(jnp.bfloat16)
        return jnp.dot(hidden, down_w, preferred_element_type=jnp.float32).astype(jnp.bfloat16)
    every = lax.map(one_expert, (gate_proj, up_proj, down_proj))
    picked = every[routes, places[:, None]]
    mixed = lax.optimization_barrier(jnp.sum(route_weights[:, :, None] * picked.astype(jnp.float32), axis=1))
    return (attn32 + mixed).astype(jnp.bfloat16)
```

```python
import jax
import jax.numpy as jnp
from jax import lax
from jax.sharding import Mesh, PartitionSpec as P

LAT = 256
VD = 128
TOP = 8
NZ, NY, NC = 4, 2, 2


score_scale = 0.0722


def local(
    queries,
    kv_latent,
    value_up,
    out_proj,
    norm_gain,
    gate_proj,
    up_proj,
    down_proj,
    routes,
    route_weights,
):
    tok, heads, width = queries.shape
    query_place = lax.axis_index("expert") * tok + jnp.arange(tok)
    piece = lax.all_gather(kv_latent, "expert", axis=0, tiled=True)
    running = jnp.full((tok, heads), -1e30, jnp.float32)
    count = piece.shape[0]
    scores = (
        jnp.einsum("shc,tc->sht", queries, piece, preferred_element_type=jnp.float32) * score_scale
    )
    key_place = jnp.arange(count)
    allowed = (query_place[:, None] >= key_place[None, :])[:, None, :]
    scores = jnp.where(allowed, scores, -1e30)
    newer = jnp.maximum(running, jnp.max(scores, axis=-1))
    expo = jnp.where(allowed, jnp.exp(scores - newer[..., None]), 0.0)
    total = jnp.sum(expo, axis=-1)
    update = jnp.einsum(
        "sht,tc->shc", expo.astype(jnp.bfloat16), piece[:, :LAT], preferred_element_type=jnp.float32
    )
    running, total, acc = (newer, total, update)
    latent_out = (acc / total[..., None]).astype(jnp.bfloat16)
    lifted = jnp.einsum(
        "shc,hcv->shv",
        latent_out,
        lax.all_gather(value_up, "expert", axis=1, tiled=True),
        preferred_element_type=jnp.float32,
    )
    flat_heads = lifted.astype(jnp.bfloat16).reshape(tok, heads * VD)
    partial_cols = jnp.dot(
        lax.all_gather(flat_heads, "expert", axis=0, tiled=True),
        out_proj,
        preferred_element_type=jnp.float32,
    )
    wide_rows = lax.all_to_all(
        partial_cols.astype(jnp.bfloat16), "expert", split_axis=0, concat_axis=1, tiled=True
    ).astype(partial_cols.dtype)
    attn = lax.psum_scatter(
        wide_rows.astype(jnp.bfloat16), "tensor", scatter_dimension=0, tiled=True
    )
    attn32 = attn.astype(jnp.float32)
    scale = lax.rsqrt(jnp.mean(attn32 * attn32, axis=-1, keepdims=True) + 1e-06)
    normed = (attn32 * scale * norm_gain).astype(jnp.bfloat16)
    rows = routes.shape[0]
    experts = lax.axis_size("expert") * gate_proj.shape[0]
    capacity = min(rows, max(2, 5 * rows * TOP // (4 * experts)))
    width_d = normed.shape[1]
    flat_routes = routes.reshape(-1)
    onehot = (flat_routes[:, None] == jnp.arange(experts)[None, :]).astype(jnp.int32)
    before = jnp.cumsum(onehot, axis=0) - onehot
    slot = jnp.sum(before * onehot, axis=1).reshape(rows, TOP)
    target = routes * capacity + slot
    slot_ids = jnp.arange(experts * capacity)
    placing = jnp.sum(
        (target[None, :, :] == slot_ids[:, None, None]).astype(jnp.int32), axis=2
    ).astype(jnp.bfloat16)
    outbound = jnp.dot(placing, normed, preferred_element_type=jnp.float32).astype(jnp.bfloat16)
    arrived = lax.all_to_all(
        outbound.reshape(experts, capacity, width_d),
        "expert",
        split_axis=0,
        concat_axis=0,
        tiled=True,
    )
    both_halves = lax.all_gather(arrived, "tensor", axis=0, tiled=True).reshape(-1, width_d)
    gate = jnp.dot(both_halves, gate_proj[0], preferred_element_type=jnp.float32)
    upper = jnp.dot(both_halves, up_proj[0], preferred_element_type=jnp.float32)
    hidden = (jax.nn.silu(gate) * upper).astype(jnp.bfloat16)
    down_terms = jnp.dot(hidden, down_proj[0], preferred_element_type=jnp.float32)
    expert_out = lax.psum_scatter(
        down_terms.astype(jnp.bfloat16), "tensor", scatter_dimension=0, tiled=True
    )
    back = lax.all_to_all(
        expert_out.reshape(experts, capacity, width_d),
        "expert",
        split_axis=0,
        concat_axis=0,
        tiled=True,
    )
    picked = back.reshape(-1, width_d)[target]
    mixed = jnp.sum(route_weights[:, :, None] * picked.astype(jnp.float32), axis=1)
    return (attn32 + mixed).astype(jnp.bfloat16)


def shift_z(value):
    return lax.ppermute(value, "z", [(i, (i + 1) % NZ) for i in range(NZ)])


def swap_y(value):
    return lax.ppermute(value, "y", [(0, 1), (1, 0)])


def swap_core(value):
    return lax.ppermute(value, "core", [(0, 1), (1, 0)])


def ring(block):
    pieces = []
    for r in range(NZ):
        pieces.append((block, swap_y(block)))
        if r < NZ - 1:
            block = shift_z(block)
    return pieces


def boxed(
    queries,
    kv_latent,
    value_up,
    out_proj,
    norm_gain,
    gate_proj,
    up_proj,
    down_proj,
    routes,
    route_weights,
):
    f32, b16 = jnp.float32, jnp.bfloat16
    tok, heads, width = queries.shape
    z, y, core = (lax.axis_index(name) for name in ("z", "y", "core"))
    place = (z * NY + y) * NC + core
    experts = NZ * NY * NC
    whole = ("z", "y", "core")

    def origin(d, r, b):
        return (((z - r) % NZ) * NY + (y ^ b)) * NC + (core ^ d)

    dense = jnp.sum(
        jnp.where(
            routes[:, :, None] == jnp.arange(experts)[None, None, :], route_weights[:, :, None], 0.0
        ),
        axis=1,
    )
    keys = lax.all_gather(kv_latent, whole, axis=0, tiled=True)
    dense_all = lax.all_gather(dense, whole, axis=0, tiled=True)

    lift_rows = jnp.concatenate([p for pair in ring(value_up) for p in pair], axis=1)
    lift = jnp.concatenate([lift_rows, swap_core(lift_rows)], axis=1)
    part = value_up.shape[1]
    order = jnp.stack([origin(d, r, b) for d in range(NC) for r in range(NZ) for b in range(NY)])
    lat_order = (order[:, None] * part + jnp.arange(part)[None, :]).reshape(-1)
    turn = (jnp.arange(LAT)[:, None] == lat_order[None, :]).astype(b16)
    values = jnp.dot(keys[:, :LAT], turn, preferred_element_type=f32).astype(b16)
    columns = jnp.concatenate([out_proj, swap_core(out_proj)], axis=1)

    query_place = place * tok + jnp.arange(tok)
    scores = jnp.einsum("shc,tc->sht", queries, keys, preferred_element_type=f32) * score_scale
    allowed = (query_place[:, None] >= jnp.arange(keys.shape[0])[None, :])[:, None, :]
    scores = jnp.where(allowed, scores, -1e30)
    top = jnp.max(scores, axis=-1)
    expo = jnp.where(allowed, jnp.exp(scores - top[..., None]), 0.0)
    total = jnp.sum(expo, axis=-1)
    acc = jnp.einsum("sht,tc->shc", expo.astype(b16), values, preferred_element_type=f32)
    latent_out = (acc / total[..., None]).astype(b16)
    lifted = jnp.einsum("shc,hcv->shv", latent_out, lift, preferred_element_type=f32)
    flat_heads = lifted.astype(b16).reshape(tok, heads * VD)

    strips = [
        [jnp.dot(p, columns, preferred_element_type=f32).astype(b16) for p in pair]
        for pair in ring(flat_heads)
    ]
    strips = jnp.stack([s for pair in strips for s in pair])
    chips = NZ * NY
    ids = jnp.arange(chips)
    here = ((z - ids // NY) % NZ) * NY + (y ^ (ids % NY))
    sent = jnp.take(strips, here, axis=0)
    got = lax.all_to_all(sent, ("z", "y"), split_axis=0, concat_axis=0, tiled=True)
    cols = out_proj.shape[1]
    got = got.reshape(chips, tok, NC, cols)
    got = jnp.where(core == 0, got, got[:, :, ::-1])
    attn32 = jnp.transpose(got, (1, 0, 2, 3)).reshape(tok, -1).astype(f32)
    scale = lax.rsqrt(jnp.mean(attn32 * attn32, axis=-1, keepdims=True) + 1e-06)
    normed = (attn32 * scale * norm_gain).astype(b16)

    width_d = normed.shape[1]
    mine = jnp.take(dense_all, place, axis=1).reshape(experts, tok)
    by_chunk = jnp.stack(
        [origin(d, r, b) for r in range(NZ) for d in range(NC) for b in range(NY)]
    )
    shares = jnp.take(mine, by_chunk, axis=0).reshape(NZ, NC * NY * tok, 1)

    def expert(block, share):
        gate = jnp.dot(block, gate_proj[0], preferred_element_type=f32)
        upper = jnp.dot(block, up_proj[0], preferred_element_type=f32)
        hidden = (jax.nn.silu(gate) * upper).astype(b16)
        return share * jnp.dot(hidden, down_proj[0], preferred_element_type=f32)

    sums = []
    for r, pair in enumerate(ring(normed)):
        own = jnp.concatenate(pair, axis=0)
        block = jnp.concatenate([own, swap_core(own)], axis=0)
        out = expert(block, shares[r])
        half = NY * tok
        out = out[:half] + swap_core(out[half:].astype(b16)).astype(f32)
        sums.append(out[:tok] + swap_y(out[tok:].astype(b16)).astype(f32))
    acc = sums[1]
    for r in (2, 3, 0):
        acc = shift_z(acc.astype(b16)).astype(f32) + sums[r]
    return (attn32 + acc).astype(b16)


def solution(mesh):
    names = "expert"
    body = local
    if mesh.shape["expert"] == NZ * NY * NC and mesh.shape["tensor"] == 1:
        groups = mesh.shape["groups"]
        mesh = Mesh(
            mesh.devices.reshape(groups, NZ, NY, NC, 1), ("groups", "z", "y", "core", "tensor")
        )
        names = ("z", "y", "core")
        body = boxed
    every = ("groups",) + (names if isinstance(names, tuple) else (names,))
    in_specs = (
        P(every, "tensor", None),
        P(every, None),
        P("tensor", names, None),
        P("tensor", names),
        P(),
        P(names, None, "tensor"),
        P(names, None, "tensor"),
        P(names, "tensor", None),
        P(every + ("tensor",), None),
        P(every + ("tensor",), None),
    )
    out_specs = P(every + ("tensor",), None)
    return jax.shard_map(body, mesh=mesh, in_specs=in_specs, out_specs=out_specs, check_vma=False)
```

```python
import jax
import jax.numpy as jnp
from jax import lax
from jax.experimental import pallas as pl
from jax.experimental.pallas import tpu as pltpu
from jax.sharding import Mesh, PartitionSpec as P

LAT = 256
VD = 128
TOP = 8
NZ, NY, NC = 4, 2, 2


score_scale = 0.0722


def local(
    queries,
    kv_latent,
    value_up,
    out_proj,
    norm_gain,
    gate_proj,
    up_proj,
    down_proj,
    routes,
    route_weights,
):
    tok, heads, width = queries.shape
    query_place = lax.axis_index("expert") * tok + jnp.arange(tok)
    piece = lax.all_gather(kv_latent, "expert", axis=0, tiled=True)
    running = jnp.full((tok, heads), -1e30, jnp.float32)
    count = piece.shape[0]
    scores = (
        jnp.einsum("shc,tc->sht", queries, piece, preferred_element_type=jnp.float32) * score_scale
    )
    key_place = jnp.arange(count)
    allowed = (query_place[:, None] >= key_place[None, :])[:, None, :]
    scores = jnp.where(allowed, scores, -1e30)
    newer = jnp.maximum(running, jnp.max(scores, axis=-1))
    expo = jnp.where(allowed, jnp.exp(scores - newer[..., None]), 0.0)
    total = jnp.sum(expo, axis=-1)
    update = jnp.einsum(
        "sht,tc->shc", expo.astype(jnp.bfloat16), piece[:, :LAT], preferred_element_type=jnp.float32
    )
    running, total, acc = (newer, total, update)
    latent_out = (acc / total[..., None]).astype(jnp.bfloat16)
    lifted = jnp.einsum(
        "shc,hcv->shv",
        latent_out,
        lax.all_gather(value_up, "expert", axis=1, tiled=True),
        preferred_element_type=jnp.float32,
    )
    flat_heads = lifted.astype(jnp.bfloat16).reshape(tok, heads * VD)
    partial_cols = jnp.dot(
        lax.all_gather(flat_heads, "expert", axis=0, tiled=True),
        out_proj,
        preferred_element_type=jnp.float32,
    )
    wide_rows = lax.all_to_all(
        partial_cols.astype(jnp.bfloat16), "expert", split_axis=0, concat_axis=1, tiled=True
    ).astype(partial_cols.dtype)
    attn = lax.psum_scatter(
        wide_rows.astype(jnp.bfloat16), "tensor", scatter_dimension=0, tiled=True
    )
    attn32 = attn.astype(jnp.float32)
    scale = lax.rsqrt(jnp.mean(attn32 * attn32, axis=-1, keepdims=True) + 1e-06)
    normed = (attn32 * scale * norm_gain).astype(jnp.bfloat16)
    rows = routes.shape[0]
    experts = lax.axis_size("expert") * gate_proj.shape[0]
    capacity = min(rows, max(2, 5 * rows * TOP // (4 * experts)))
    width_d = normed.shape[1]
    flat_routes = routes.reshape(-1)
    onehot = (flat_routes[:, None] == jnp.arange(experts)[None, :]).astype(jnp.int32)
    before = jnp.cumsum(onehot, axis=0) - onehot
    slot = jnp.sum(before * onehot, axis=1).reshape(rows, TOP)
    target = routes * capacity + slot
    slot_ids = jnp.arange(experts * capacity)
    placing = jnp.sum(
        (target[None, :, :] == slot_ids[:, None, None]).astype(jnp.int32), axis=2
    ).astype(jnp.bfloat16)
    outbound = jnp.dot(placing, normed, preferred_element_type=jnp.float32).astype(jnp.bfloat16)
    arrived = lax.all_to_all(
        outbound.reshape(experts, capacity, width_d),
        "expert",
        split_axis=0,
        concat_axis=0,
        tiled=True,
    )
    both_halves = lax.all_gather(arrived, "tensor", axis=0, tiled=True).reshape(-1, width_d)
    gate = jnp.dot(both_halves, gate_proj[0], preferred_element_type=jnp.float32)
    upper = jnp.dot(both_halves, up_proj[0], preferred_element_type=jnp.float32)
    hidden = (jax.nn.silu(gate) * upper).astype(jnp.bfloat16)
    down_terms = jnp.dot(hidden, down_proj[0], preferred_element_type=jnp.float32)
    expert_out = lax.psum_scatter(
        down_terms.astype(jnp.bfloat16), "tensor", scatter_dimension=0, tiled=True
    )
    back = lax.all_to_all(
        expert_out.reshape(experts, capacity, width_d),
        "expert",
        split_axis=0,
        concat_axis=0,
        tiled=True,
    )
    picked = back.reshape(-1, width_d)[target]
    mixed = jnp.sum(route_weights[:, :, None] * picked.astype(jnp.float32), axis=1)
    return (attn32 + mixed).astype(jnp.bfloat16)


CHIPS = [(r, b) for r in range(NZ) for b in range(NY)]
NT = (((1,), (1,)), ((), ()))
F32, B16 = jnp.float32, jnp.bfloat16


def shift_z(value):
    return lax.ppermute(value, "z", [(i, (i + 1) % NZ) for i in range(NZ)])


def swap_y(value):
    return lax.ppermute(value, "y", [(0, 1), (1, 0)])


def swap_core(value):
    return lax.ppermute(value, "core", [(0, 1), (1, 0)])


def hand_back(value, r, b):
    if r == 0 and b == 0:
        return value
    pairs = [
        (z * NY + y, ((z - r) % NZ) * NY + (y ^ b)) for z in range(NZ) for y in range(NY)
    ]
    return lax.ppermute(value, ("z", "y"), pairs)


def ring(block):
    pieces = {}
    for r in range(NZ):
        pieces[r, 0] = block
        pieces[r, 1] = swap_y(block)
        if r < NZ - 1:
            block = shift_z(block)
    return pieces


def whole_block(shape):
    return pl.BlockSpec(shape, lambda i, *_: (0,) * len(shape))


def attend(q_own, q_other, k_own, k_other, query_place, key_place):
    heads, tok, width = q_own.shape
    half, wide = k_own.shape
    rows = 2 * tok
    hb = 2
    turn = score_scale * 1.4426950408889634

    def kernel(qp, kp, qo, qx, ko, kx, out, bias):
        @pl.when(pl.program_id(0) == 0)
        def _():
            for j in range(hb):
                bias[j * rows : (j + 1) * rows] = jnp.where(qp[...] >= kp[...], 0.0, -1e30)

        q = jnp.concatenate([ref[j] for j in range(hb) for ref in (qo, qx)], axis=0)
        s0 = lax.dot_general(q, ko[:, :width], NT, preferred_element_type=F32) + bias[:, :half]
        s1 = lax.dot_general(q, kx[:, :width], NT, preferred_element_type=F32) + bias[:, half:]
        top = jnp.maximum(
            jnp.max(s0, axis=-1, keepdims=True), jnp.max(s1, axis=-1, keepdims=True)
        )
        p0 = jnp.exp2((s0 - top) * turn)
        p1 = jnp.exp2((s1 - top) * turn)
        total = jnp.sum(p0, axis=-1, keepdims=True) + jnp.sum(p1, axis=-1, keepdims=True)
        acc = jnp.dot(p0.astype(B16), ko[:, :LAT], preferred_element_type=F32)
        acc = acc + jnp.dot(p1.astype(B16), kx[:, :LAT], preferred_element_type=F32)
        latent = (acc / total).astype(B16)
        for j in range(hb):
            out[j] = latent[j * rows : (j + 1) * rows]

    return pl.pallas_call(
        kernel,
        grid=(heads // hb,),
        in_specs=[
            whole_block((rows, 1)),
            whole_block((1, 2 * half)),
            pl.BlockSpec((hb, tok, width), lambda i: (i, 0, 0)),
            pl.BlockSpec((hb, tok, width), lambda i: (i, 0, 0)),
            whole_block((half, wide)),
            whole_block((half, wide)),
        ],
        out_specs=pl.BlockSpec((hb, rows, LAT), lambda i: (i, 0, 0)),
        out_shape=jax.ShapeDtypeStruct((heads, rows, LAT), B16),
        scratch_shapes=[pltpu.VMEM((hb * rows, 2 * half), F32)],
        compiler_params=pltpu.CompilerParams(vmem_limit_bytes=32 << 20),
        cost_estimate=pl.CostEstimate(
            flops=2 * heads * rows * 2 * half * (width + LAT),
            bytes_accessed=8 << 20,
            transcendentals=heads * rows * 2 * half,
        ),
        name="attend",
    )(query_place, key_place, q_own, q_other, k_own, k_other)


def raise_values(latent, pieces, at):
    heads, rows, _ = latent.shape
    hb = 8
    part = pieces[0, 0].shape[1]

    def kernel(where, lat, *refs):
        parts, out, lift = refs[: len(CHIPS)], refs[-2], refs[-1]
        for n, ref in enumerate(parts):
            lift[:, pl.ds(pl.multiple_of(where[n] * part, part), part), :] = ref[...]
        for j in range(hb):
            out[:, j * VD : (j + 1) * VD] = jnp.dot(
                lat[j], lift[j], preferred_element_type=F32
            ).astype(B16)

    return pl.pallas_call(
        kernel,
        grid_spec=pltpu.PrefetchScalarGridSpec(
            num_scalar_prefetch=1,
            grid=(heads // hb,),
            in_specs=[pl.BlockSpec((hb, rows, LAT), lambda i, _: (i, 0, 0))]
            + [pl.BlockSpec((hb, part, VD), lambda i, _: (i, 0, 0))] * len(CHIPS),
            out_specs=pl.BlockSpec((rows, hb * VD), lambda i, _: (0, i)),
            scratch_shapes=[pltpu.VMEM((hb, LAT, VD), B16)],
        ),
        out_shape=jax.ShapeDtypeStruct((rows, heads * VD), B16),
        compiler_params=pltpu.CompilerParams(vmem_limit_bytes=24 << 20),
        cost_estimate=pl.CostEstimate(
            flops=2 * heads * rows * LAT * VD, bytes_accessed=6 << 20, transcendentals=0
        ),
        name="raise_values",
    )(at, latent, *[pieces[chip] for chip in CHIPS])


def normalise(strips, at, norm_gain):
    tok, cols = strips[0, 0].shape
    wide = NY * cols

    def kernel(where, gain, *refs):
        parts, attn, normed, pair, square = refs[: len(CHIPS)], *refs[-4:]
        square[...] = jnp.zeros_like(square)
        for r in range(NZ):
            low, high = parts[NY * r][...].astype(F32), parts[NY * r + 1][...].astype(F32)
            swap = jnp.full((tok, cols), where[0], jnp.int32) == 1
            pair[:, :cols] = jnp.where(swap, high, low)
            pair[:, cols:] = jnp.where(swap, low, high)
            both = pair[...]
            attn[:, pl.ds(pl.multiple_of(where[1 + r] * wide, 128), wide)] = both.astype(B16)
            square[...] += jnp.sum(both * both, axis=-1, keepdims=True)
        scale = lax.rsqrt(square[...] / (NZ * wide) + 1e-06)
        normed[...] = (attn[...].astype(F32) * scale * gain[...]).astype(B16)

    shape = jax.ShapeDtypeStruct((tok, NZ * wide), B16)
    return pl.pallas_call(
        kernel,
        grid_spec=pltpu.PrefetchScalarGridSpec(
            num_scalar_prefetch=1,
            grid=(1,),
            in_specs=[whole_block((1, NZ * wide))] + [whole_block((tok, cols))] * len(CHIPS),
            out_specs=[whole_block((tok, NZ * wide))] * 2,
            scratch_shapes=[pltpu.VMEM((tok, wide), F32), pltpu.VMEM((tok, 1), F32)],
        ),
        out_shape=[shape, shape],
        compiler_params=pltpu.CompilerParams(vmem_limit_bytes=16 << 20),
        cost_estimate=pl.CostEstimate(flops=1 << 20, bytes_accessed=2 << 20, transcendentals=0),
        name="normalise",
    )(at, norm_gain.reshape(1, -1), *[strips[chip] for chip in CHIPS])


def expert(blocks, shares, gate_proj, up_proj, down_proj):
    tok, width = blocks[0].shape
    hidden_units = gate_proj.shape[2]
    fb = 256
    n = len(blocks)
    rows = n * tok
    steps = hidden_units // fb

    def kernel(share, gate_w, up_w, down_w, *refs):
        ins, outs, x, acc = refs[:n], refs[n : 2 * n], refs[-2], refs[-1]
        step = pl.program_id(0)

        @pl.when(step == 0)
        def _():
            for j in range(n):
                x[j * tok : (j + 1) * tok] = ins[j][...]

        gate = jnp.dot(x[...], gate_w[0], preferred_element_type=F32)
        upper = jnp.dot(x[...], up_w[0], preferred_element_type=F32)
        hidden = (jax.nn.silu(gate) * upper).astype(B16)
        down = jnp.dot(hidden, down_w[0], preferred_element_type=F32)

        @pl.when(step == 0)
        def _():
            acc[...] = down

        @pl.when((step > 0) & (step < steps - 1))
        def _():
            acc[...] += down

        @pl.when(step == steps - 1)
        def _():
            out = ((acc[...] + down) * share[...]).astype(B16)
            for j in range(n):
                outs[j][...] = out[j * tok : (j + 1) * tok]

    return pl.pallas_call(
        kernel,
        grid=(steps,),
        in_specs=[
            whole_block((rows, 1)),
            pl.BlockSpec((1, width, fb), lambda i: (0, 0, i)),
            pl.BlockSpec((1, width, fb), lambda i: (0, 0, i)),
            pl.BlockSpec((1, fb, width), lambda i: (0, i, 0)),
        ]
        + [whole_block((tok, width))] * n,
        out_specs=[whole_block((tok, width))] * n,
        out_shape=[jax.ShapeDtypeStruct((tok, width), B16)] * n,
        scratch_shapes=[pltpu.VMEM((rows, width), B16), pltpu.VMEM((rows, width), F32)],
        compiler_params=pltpu.CompilerParams(vmem_limit_bytes=40 << 20),
        cost_estimate=pl.CostEstimate(
            flops=6 * rows * width * hidden_units, bytes_accessed=26 << 20, transcendentals=0
        ),
        name="expert",
    )(shares, gate_proj, up_proj, down_proj, *blocks)


def boxed(
    queries,
    kv_latent,
    value_up,
    out_proj,
    norm_gain,
    gate_proj,
    up_proj,
    down_proj,
    routes,
    route_weights,
):
    tok, heads, width = queries.shape
    z, y, core = (lax.axis_index(name) for name in ("z", "y", "core"))
    experts = NZ * NY * NC
    place = (z * NY + y) * NC + core
    first = core == 0
    hh = heads // NC

    dense = jnp.sum(
        jnp.where(
            routes[:, :, None] == jnp.arange(experts)[None, None, :], route_weights[:, :, None], 0.0
        ),
        axis=1,
    )
    high = dense.astype(B16)
    low = (dense - high.astype(F32)).astype(B16)
    pack = jnp.concatenate([kv_latent, high, low], axis=1)
    pack = jnp.broadcast_to(pack[None], (len(CHIPS),) + pack.shape)
    k_own = lax.all_to_all(pack, ("z", "y"), split_axis=0, concat_axis=0, tiled=True)
    k_own = k_own.reshape(-1, k_own.shape[-1])
    k_other = swap_core(k_own)

    by_head = jnp.transpose(queries, (1, 0, 2)).reshape(NC, hh, tok, width)
    q_own = lax.dynamic_index_in_dim(by_head, core, 0, keepdims=False)
    q_other = swap_core(lax.dynamic_index_in_dim(by_head, 1 - core, 0, keepdims=False))
    lift = value_up.reshape(NC, hh, -1, VD)
    lift_own = lax.dynamic_index_in_dim(lift, core, 0, keepdims=False)
    lift_other = swap_core(lax.dynamic_index_in_dim(lift, 1 - core, 0, keepdims=False))
    lift = jnp.concatenate(
        [jnp.where(first, lift_own, lift_other), jnp.where(first, lift_other, lift_own)], axis=1
    )
    lift_pieces = ring(lift)

    kk = out_proj.shape[0] // NC
    proj_own = lax.dynamic_slice_in_dim(out_proj, core * kk, kk, 0)
    proj_other = swap_core(lax.dynamic_slice_in_dim(out_proj, (1 - core) * kk, kk, 0))
    columns = jnp.concatenate(
        [jnp.where(first, proj_own, proj_other), jnp.where(first, proj_other, proj_own)], axis=1
    )

    steps = jnp.arange(tok)
    query_place = jnp.concatenate([place * tok + steps, (place ^ 1) * tok + steps])[:, None]
    chip_rows = jnp.arange(NZ * NY)[:, None] * (NC * tok) + steps[None, :]
    key_place = jnp.concatenate(
        [(chip_rows + core * tok).reshape(-1), (chip_rows + (1 - core) * tok).reshape(-1)]
    )[None, :]
    latent = attend(q_own, q_other, k_own, k_other, query_place, key_place)
    down_chips = jnp.stack([((z - r) % NZ) * NY + (y ^ b) for r, b in CHIPS])
    flat_heads = raise_values(latent, lift_pieces, down_chips)

    strips = {}
    for chip, piece in ring(flat_heads).items():
        part = jnp.dot(piece, columns, preferred_element_type=F32)
        strip = (part[:tok] + swap_core(part[tok:].astype(B16)).astype(F32)).astype(B16)
        strips[chip] = hand_back(strip, *chip)
    at = jnp.stack([y] + [(z + r) % NZ for r in range(NZ)])
    attn, normed = normalise(strips, at, norm_gain)

    def mine(pack):
        flat = pack[:, width:].astype(F32).reshape(len(CHIPS), tok, 2, experts).sum(axis=2)
        return jnp.take(flat, place, axis=2)

    shares = [mine(k_own), mine(k_other)]

    sums = {}
    pieces = ring(normed)
    for r in range(NZ):
        blocks = [pieces[r, b] for b in range(NY)]
        blocks += [swap_core(block) for block in blocks]
        share = jnp.concatenate(
            [
                lax.dynamic_index_in_dim(shares[d], ((z - r) % NZ) * NY + (y ^ b), 0, False)
                for d in range(NC)
                for b in range(NY)
            ]
        )[:, None]
        out = expert(blocks, share, gate_proj, up_proj, down_proj)
        far = out[1].astype(F32) + swap_core(out[3]).astype(F32)
        near = out[0].astype(F32) + swap_core(out[2]).astype(F32)
        sums[r] = near + swap_y(far.astype(B16)).astype(F32)
    acc = sums[1]
    for r in (2, 3, 0):
        acc = shift_z(acc.astype(B16)).astype(F32) + sums[r]
    return (attn.astype(F32) + acc).astype(B16)


def solution(mesh):
    names = ("expert",)
    body = local
    if mesh.shape["expert"] == NZ * NY * NC and mesh.shape["tensor"] == 1:
        groups = mesh.shape["groups"]
        mesh = Mesh(
            mesh.devices.reshape(groups, NZ, NY, NC, 1), ("groups", "z", "y", "core", "tensor")
        )
        names = ("z", "y", "core")
        body = boxed
    every = ("groups",) + names
    in_specs = (
        P(every, "tensor", None),
        P(every, None),
        P("tensor", names, None),
        P("tensor", names),
        P(),
        P(names, None, "tensor"),
        P(names, None, "tensor"),
        P(names, "tensor", None),
        P(every + ("tensor",), None),
        P(every + ("tensor",), None),
    )
    out_specs = P(every + ("tensor",), None)
    return jax.shard_map(body, mesh=mesh, in_specs=in_specs, out_specs=out_specs, check_vma=False)
```

```python
import jax
import jax.numpy as jnp
from jax import lax
from jax.experimental import pallas as pl
from jax.experimental.pallas import tpu as pltpu
from jax.sharding import Mesh, PartitionSpec as P

LAT = 256
VD = 128
TOP = 8
NZ, NY, NC = 4, 2, 2


score_scale = 0.0722


def local(
    queries,
    kv_latent,
    value_up,
    out_proj,
    norm_gain,
    gate_proj,
    up_proj,
    down_proj,
    routes,
    route_weights,
):
    tok, heads, width = queries.shape
    query_place = lax.axis_index("expert") * tok + jnp.arange(tok)
    piece = lax.all_gather(kv_latent, "expert", axis=0, tiled=True)
    running = jnp.full((tok, heads), -1e30, jnp.float32)
    count = piece.shape[0]
    scores = (
        jnp.einsum("shc,tc->sht", queries, piece, preferred_element_type=jnp.float32) * score_scale
    )
    key_place = jnp.arange(count)
    allowed = (query_place[:, None] >= key_place[None, :])[:, None, :]
    scores = jnp.where(allowed, scores, -1e30)
    newer = jnp.maximum(running, jnp.max(scores, axis=-1))
    expo = jnp.where(allowed, jnp.exp(scores - newer[..., None]), 0.0)
    total = jnp.sum(expo, axis=-1)
    update = jnp.einsum(
        "sht,tc->shc", expo.astype(jnp.bfloat16), piece[:, :LAT], preferred_element_type=jnp.float32
    )
    running, total, acc = (newer, total, update)
    latent_out = (acc / total[..., None]).astype(jnp.bfloat16)
    lifted = jnp.einsum(
        "shc,hcv->shv",
        latent_out,
        lax.all_gather(value_up, "expert", axis=1, tiled=True),
        preferred_element_type=jnp.float32,
    )
    flat_heads = lifted.astype(jnp.bfloat16).reshape(tok, heads * VD)
    partial_cols = jnp.dot(
        lax.all_gather(flat_heads, "expert", axis=0, tiled=True),
        out_proj,
        preferred_element_type=jnp.float32,
    )
    wide_rows = lax.all_to_all(
        partial_cols.astype(jnp.bfloat16), "expert", split_axis=0, concat_axis=1, tiled=True
    ).astype(partial_cols.dtype)
    attn = lax.psum_scatter(
        wide_rows.astype(jnp.bfloat16), "tensor", scatter_dimension=0, tiled=True
    )
    attn32 = attn.astype(jnp.float32)
    scale = lax.rsqrt(jnp.mean(attn32 * attn32, axis=-1, keepdims=True) + 1e-06)
    normed = (attn32 * scale * norm_gain).astype(jnp.bfloat16)
    rows = routes.shape[0]
    experts = lax.axis_size("expert") * gate_proj.shape[0]
    capacity = min(rows, max(2, 5 * rows * TOP // (4 * experts)))
    width_d = normed.shape[1]
    flat_routes = routes.reshape(-1)
    onehot = (flat_routes[:, None] == jnp.arange(experts)[None, :]).astype(jnp.int32)
    before = jnp.cumsum(onehot, axis=0) - onehot
    slot = jnp.sum(before * onehot, axis=1).reshape(rows, TOP)
    target = routes * capacity + slot
    slot_ids = jnp.arange(experts * capacity)
    placing = jnp.sum(
        (target[None, :, :] == slot_ids[:, None, None]).astype(jnp.int32), axis=2
    ).astype(jnp.bfloat16)
    outbound = jnp.dot(placing, normed, preferred_element_type=jnp.float32).astype(jnp.bfloat16)
    arrived = lax.all_to_all(
        outbound.reshape(experts, capacity, width_d),
        "expert",
        split_axis=0,
        concat_axis=0,
        tiled=True,
    )
    both_halves = lax.all_gather(arrived, "tensor", axis=0, tiled=True).reshape(-1, width_d)
    gate = jnp.dot(both_halves, gate_proj[0], preferred_element_type=jnp.float32)
    upper = jnp.dot(both_halves, up_proj[0], preferred_element_type=jnp.float32)
    hidden = (jax.nn.silu(gate) * upper).astype(jnp.bfloat16)
    down_terms = jnp.dot(hidden, down_proj[0], preferred_element_type=jnp.float32)
    expert_out = lax.psum_scatter(
        down_terms.astype(jnp.bfloat16), "tensor", scatter_dimension=0, tiled=True
    )
    back = lax.all_to_all(
        expert_out.reshape(experts, capacity, width_d),
        "expert",
        split_axis=0,
        concat_axis=0,
        tiled=True,
    )
    picked = back.reshape(-1, width_d)[target]
    mixed = jnp.sum(route_weights[:, :, None] * picked.astype(jnp.float32), axis=1)
    return (attn32 + mixed).astype(jnp.bfloat16)


CHIPS = [(r, b) for r in range(NZ) for b in range(NY)]
NT = (((1,), (1,)), ((), ()))
F32, B16 = jnp.float32, jnp.bfloat16
WHOLE = pl.BlockSpec(memory_space=pltpu.VMEM)
barrier = lax.optimization_barrier


def shift_z(value, by=1):
    return lax.ppermute(value, "z", [(i, (i + by) % NZ) for i in range(NZ)])


def swap_y(value):
    return lax.ppermute(value, "y", [(0, 1), (1, 0)])


def swap_core(value):
    return lax.ppermute(value, "core", [(0, 1), (1, 0)])


def hand_back(value, r, b):
    if r == 0 and b == 0:
        return value
    pairs = [
        (z * NY + y, ((z - r) % NZ) * NY + (y ^ b)) for z in range(NZ) for y in range(NY)
    ]
    return lax.ppermute(value, ("z", "y"), pairs)


def call(kernel, outs, scratch, limit, flops, name, *args):
    size = sum(a.size * a.dtype.itemsize for a in args)
    return pl.pallas_call(
        kernel,
        in_specs=[
            pl.BlockSpec(memory_space=pltpu.SMEM) if a.ndim == 1 else WHOLE for a in args
        ],
        out_specs=[WHOLE] * len(outs),
        out_shape=[
            jax.ShapeDtypeStruct(o, B16) if isinstance(o, tuple) else o for o in outs
        ],
        scratch_shapes=scratch,
        compiler_params=pltpu.CompilerParams(vmem_limit_bytes=limit << 20),
        cost_estimate=pl.CostEstimate(flops=flops, bytes_accessed=size, transcendentals=0),
        name=name,
    )(*args)


def pack_keys(kv_latent, routes, route_weights, experts):
    tok, width = kv_latent.shape

    def kernel(kv, routed, weight, out):
        dense = jnp.zeros((experts, tok), F32)
        number = lax.broadcasted_iota(jnp.int32, (experts, tok), 0)
        for k in range(TOP):
            dense = dense + jnp.where(routed[k : k + 1] == number, weight[k : k + 1], 0.0)
        high = dense.astype(B16)
        low = (dense - high.astype(F32)).astype(B16)
        same = lax.broadcasted_iota(jnp.int32, (tok, tok), 0) == lax.broadcasted_iota(
            jnp.int32, (tok, tok), 1
        )
        eye = jnp.where(same, 1.0, 0.0).astype(B16)
        out[:, :width] = kv[...]
        for n, term in enumerate((high, low)):
            at = width + n * experts
            out[:, at : at + experts] = lax.dot_general(
                eye, term, NT, preferred_element_type=F32
            ).astype(B16)

    return call(
        kernel,
        [(tok, width + 2 * experts)],
        [],
        2,
        1 << 20,
        "pack_keys",
        kv_latent,
        routes.T,
        route_weights.T,
    )[0]


def split_heads(where, queries):
    tok, heads, width = queries.shape
    half = heads // NC

    def kernel(where, q, own, send):
        for at, out in ((where[0], own), (1 - where[0], send)):
            first = pl.multiple_of(at * half, half)
            out[...] = jnp.swapaxes(q[:, pl.ds(first, half), :], 0, 1)

    shapes = [(half, tok, width)] * 2
    return call(kernel, shapes, [], 16, 1 << 16, "split_heads", where, queries)


def split_values(where, value_up):
    heads, part, _ = value_up.shape
    half = heads // NC

    def kernel(where, v, own, send):
        for at, out in ((where[0], own), (1 - where[0], send)):
            out[...] = v[pl.ds(pl.multiple_of(at * half, half), half)]

    shapes = [(half, part, VD)] * 2
    return call(kernel, shapes, [], 2, 1 << 16, "split_values", where, value_up)


def join_cores(where, own, other):
    heads, part, width = own.shape

    def kernel(where, a, b, out):
        out[:, pl.ds(pl.multiple_of(where[0] * part, part), part), :] = a[...]
        out[:, pl.ds(pl.multiple_of((1 - where[0]) * part, part), part), :] = b[...]

    return call(
        kernel, [(heads, 2 * part, width)], [], 4, 1 << 10, "join_cores", where, own, other
    )[0]


def stack_rows(blocks):
    rows, width = blocks[0].shape

    def kernel(*refs):
        for n, ref in enumerate(refs[:-1]):
            refs[-1][n * rows : (n + 1) * rows] = ref[...]

    return call(kernel, [(rows * len(blocks), width)], [], 2, 1 << 16, "stack_rows", *blocks)[0]


def attend(which, q_own, q_other, k_own, k_other, query_place, key_place):
    heads, tok, width = q_own.shape
    heads = heads // 2
    half = k_own.shape[0]
    rows = 2 * tok
    hb, sub = 8, 2
    turn = score_scale * 1.4426950408889634

    def kernel(qp, kp, qo, qx, ko, kx, out, bias):
        for j in range(sub):
            bias[j * rows : (j + 1) * rows] = jnp.where(qp[...] >= kp[...], 0.0, -1e30)
        first = which * heads

        def body(step, _):
            base = step * hb
            for g in range(0, hb, sub):
                q = jnp.concatenate(
                    [ref[first + base + j] for j in range(g, g + sub) for ref in (qo, qx)], axis=0
                )
                s0 = lax.dot_general(q, ko[:, :width], NT, preferred_element_type=F32)
                s1 = lax.dot_general(q, kx[:, :width], NT, preferred_element_type=F32)
                s0 = s0 + bias[:, :half]
                s1 = s1 + bias[:, half:]
                top = jnp.maximum(
                    jnp.max(s0, axis=-1, keepdims=True), jnp.max(s1, axis=-1, keepdims=True)
                )
                p0 = jnp.exp2((s0 - top) * turn)
                p1 = jnp.exp2((s1 - top) * turn)
                total = jnp.sum(p0, axis=-1, keepdims=True) + jnp.sum(p1, axis=-1, keepdims=True)
                acc = jnp.dot(p0.astype(B16), ko[:, :LAT], preferred_element_type=F32)
                acc = acc + jnp.dot(p1.astype(B16), kx[:, :LAT], preferred_element_type=F32)
                latent = (acc / total).astype(B16)
                for j in range(sub):
                    out[base + g + j] = latent[j * rows : (j + 1) * rows]
            return 0

        lax.fori_loop(0, heads // hb, body, 0)

    return call(
        kernel,
        [(heads, rows, LAT)],
        [pltpu.VMEM((sub * rows, 2 * half), F32)],
        16,
        2 * heads * rows * 2 * half * (width + LAT),
        "attend",
        query_place,
        key_place,
        q_own,
        q_other,
        k_own,
        k_other,
    )[0]


def raise_values(chips, latents, pieces):
    heads, rows, _ = latents[0].shape
    part = pieces[0].shape[1]
    n = len(latents)

    def kernel(chip, *refs):
        lat, parts, out, lift = refs[:n], refs[n:-2], refs[-2], refs[-1]
        for at, ref in enumerate(parts):
            lift[:, pl.ds(pl.multiple_of(chip[at] * part, part), part), :] = ref[...]
        for j in range(n * heads):
            out[:, j * VD : (j + 1) * VD] = jnp.dot(
                lat[j // heads][j % heads], lift[j], preferred_element_type=F32
            ).astype(B16)

    return call(
        kernel,
        [(rows, n * heads * VD)],
        [pltpu.VMEM((n * heads, LAT, VD), B16)],
        8,
        2 * n * heads * rows * LAT * VD,
        "raise_values",
        chips,
        *latents,
        *pieces,
    )[0]


def split_proj(where, flat):
    cols, rows = flat.shape
    half = rows // NC

    def kernel(where, a, own, send):
        own[...] = a[:, pl.ds(pl.multiple_of(where[0] * half, half), half)]
        send[...] = a[:, pl.ds(pl.multiple_of((1 - where[0]) * half, half), half)]

    return call(kernel, [(cols, half)] * 2, [], 4, 1 << 16, "split_proj", where, flat)


def join_proj(where, own, other):
    cols, rows = own.shape

    def kernel(where, a, b, out):
        out[pl.ds(pl.multiple_of(where[0] * cols, 16), cols), :] = a[...]
        out[pl.ds(pl.multiple_of((1 - where[0]) * cols, 16), cols), :] = b[...]

    return call(kernel, [(2 * cols, rows)], [], 4, 1 << 16, "join_proj", where, own, other)[0]


def halves(block):
    rows = block.shape[0] // 2

    def kernel(ref, low, high):
        low[...] = ref[:rows]
        high[...] = ref[rows:]

    return call(kernel, [(rows, block.shape[1])] * 2, [], 2, 1 << 16, "halves", block)


def project(columns, *parts):
    rows = sum(part.shape[0] for part in parts)
    cols, depth = columns.shape
    tok = rows // 2

    def kernel(b, *refs):
        keep, send = refs[-2:]
        piece = jnp.concatenate([ref[...] for ref in refs[:-2]], axis=0)
        part = lax.dot_general(piece, b[...], NT, preferred_element_type=F32)
        keep[...] = part[:tok]
        send[...] = part[tok:].astype(B16)

    return call(
        kernel,
        [jax.ShapeDtypeStruct((tok, cols), F32), (tok, cols)],
        [],
        6,
        2 * rows * depth * cols,
        "project",
        columns,
        *parts,
    )


def add(rows, at, *terms):
    def kernel(*refs):
        total = 0.0
        for ref in refs[:-1]:
            block = ref[...] if ref.shape[0] == rows else ref[at : at + rows]
            total = total + block.astype(F32)
        refs[-1][...] = total.astype(B16)

    shape = (rows, terms[0].shape[1])
    return call(kernel, [shape], [], 4, rows * shape[1], "add", *terms)[0]


def normalise(chips, strips, norm_gain):
    tok, cols = strips[0].shape
    wide = len(CHIPS) * cols

    def kernel(chip, gain, *refs):
        parts, attn, normed, stage, full = refs[: len(CHIPS)], *refs[-4:]
        for n, ref in enumerate(parts):
            stage[chip[n]] = ref[...].astype(F32)
        for n in range(len(CHIPS)):
            full[:, n * cols : (n + 1) * cols] = stage[n]
        value = full[...]
        attn[...] = value.astype(B16)
        scale = lax.rsqrt(jnp.mean(value * value, axis=-1, keepdims=True) + 1e-06)
        normed[...] = (value * scale * gain[...]).astype(B16)

    return call(
        kernel,
        [(tok, wide)] * 2,
        [pltpu.VMEM((len(CHIPS), tok, cols), F32), pltpu.VMEM((tok, wide), F32)],
        8,
        1 << 20,
        "normalise",
        chips,
        norm_gain.reshape(1, -1),
        *strips,
    )


def load(weight):
    def kernel(source, out, sem):
        copy = pltpu.make_async_copy(source, out, sem)
        copy.start()
        copy.wait()

    return pl.pallas_call(
        kernel,
        in_specs=[pl.BlockSpec(memory_space=pltpu.HBM)],
        out_specs=WHOLE,
        out_shape=jax.ShapeDtypeStruct(weight.shape, weight.dtype),
        scratch_shapes=[pltpu.SemaphoreType.DMA],
        compiler_params=pltpu.CompilerParams(vmem_limit_bytes=2 << 20),
        cost_estimate=pl.CostEstimate(flops=0, bytes_accessed=weight.size * 2, transcendentals=0),
        name="load",
    )(weight)


def expert(r, where, k_own, k_other, blocks, weights):
    tok, width = blocks[0].shape
    units = weights[0].shape[2]
    fb, nb = 256, 512
    n = len(blocks)
    rows = n * tok
    side = NY * tok
    dense = k_own.shape[1]
    experts = len(CHIPS) * NC

    def kernel(where, ko, kx, gate_w, up_w, down_w, *refs):
        ins, outs, x, hidden, share = refs[:n], refs[n : n + NC], *refs[-3:]
        lane = lax.broadcasted_iota(jnp.int32, (tok, 2 * experts), 1)
        mine = (lane == where[1]) | (lane == where[1] + experts)
        for d, ref in enumerate((ko, kx)):
            for b in range(NY):
                at = (b * NZ + r) * tok
                table = ref[at : at + tok, dense - 2 * experts :].astype(F32)
                to = d * side + b * tok
                share[to : to + tok] = jnp.sum(
                    jnp.where(mine, table, 0.0), axis=-1, keepdims=True
                )
        for j in range(n):
            x[j * tok : (j + 1) * tok] = ins[j][...]
        for f in range(0, units, fb):
            gate = jnp.dot(x[...], gate_w[0, :, f : f + fb], preferred_element_type=F32)
            upper = jnp.dot(x[...], up_w[0, :, f : f + fb], preferred_element_type=F32)
            hidden[:, f : f + fb] = (jax.nn.silu(gate) * upper).astype(B16)
        for c in range(0, width, nb):
            down = jnp.dot(hidden[...], down_w[0, :, c : c + nb], preferred_element_type=F32)
            out = (down * share[...]).astype(B16)
            for d in range(NC):
                outs[d][:, c : c + nb] = out[d * side : (d + 1) * side]

    return call(
        kernel,
        [(side, width)] * NC,
        [
            pltpu.VMEM((rows, width), B16),
            pltpu.VMEM((rows, units), B16),
            pltpu.VMEM((rows, 1), F32),
        ],
        10,
        6 * rows * width * units,
        "expert",
        where,
        k_own,
        k_other,
        *weights,
        *blocks,
    )


def boxed(
    queries,
    kv_latent,
    value_up,
    out_proj,
    norm_gain,
    gate_proj,
    up_proj,
    down_proj,
    routes,
    route_weights,
):
    tok, heads, width = queries.shape
    z, y, core = (lax.axis_index(name) for name in ("z", "y", "core"))
    experts = NZ * NY * NC
    place = (z * NY + y) * NC + core
    where = jnp.stack([core, place]).astype(jnp.int32)
    up_chips = jnp.stack([((z + r) % NZ) * NY + (y ^ b) for r, b in CHIPS])
    down_chips = jnp.stack([((z - r) % NZ) * NY + (y ^ b) for r, b in CHIPS])
    steps = jnp.arange(tok)
    query_place = jnp.concatenate([place * tok + steps, (place ^ 1) * tok + steps])[:, None]
    key_chips = jnp.stack([((z - r) % NZ) * NY + (y ^ b) for b in range(NY) for r in range(NZ)])
    chip_rows = key_chips[:, None] * (NC * tok) + steps[None, :]
    key_place = jnp.concatenate(
        [(chip_rows + core * tok).reshape(-1), (chip_rows + (1 - core) * tok).reshape(-1)]
    )[None, :]
    where, up_chips, down_chips, query_place, key_place, kv_latent = barrier(
        (where, up_chips, down_chips, query_place, key_place, kv_latent)
    )

    lift_own, lift_send = split_values(where, value_up)
    pack = pack_keys(kv_latent, routes, route_weights, experts)
    lift_own, lift_send, pack, queries, out_proj = barrier(
        (lift_own, lift_send, pack, queries, out_proj)
    )
    keys = [pack] + [shift_z(pack, r) for r in range(1, NZ)]
    lift_other = swap_core(lift_send)
    q_own, q_send = split_heads(where, queries)
    proj_own, proj_send = split_proj(where, out_proj.T)
    *keys, lift_other, q_own, q_send, proj_own, proj_send = barrier(
        (*keys, lift_other, q_own, q_send, proj_own, proj_send)
    )

    column = stack_rows(keys)
    lift = join_cores(where, lift_own, lift_other)
    column, lift = barrier((column, lift))
    beside = swap_y(column)
    up1, side0 = shift_z(lift), swap_y(lift)
    q_other = swap_core(q_send)
    proj_other = swap_core(proj_send)
    beside, up1, side0, q_other, proj_other = barrier((beside, up1, side0, q_other, proj_other))

    k_own = stack_rows([column, beside])
    up2, side1 = shift_z(up1), swap_y(up1)
    k_other = swap_core(k_own)
    columns = join_proj(where, proj_own, proj_other)
    k_other, columns = barrier((k_other, columns))
    args = (q_own, q_other, k_own, k_other, query_place, key_place)
    latent0 = attend(0, *args)
    up2, side1, latent0, q_own = barrier((up2, side1, latent0, q_own))
    up3, side2 = shift_z(up2), swap_y(up2)
    latent1 = attend(1, q_own, *args[1:])
    up3, side2, latent1 = barrier((up3, side2, latent1))
    side3 = swap_y(up3)
    lifts = (lift, side0, up1, side1, up2, side2, up3, side3)
    block = raise_values(down_chips, (latent0, latent1), lifts)

    strips = {}

    def send_home(chip, *parts):
        kept, sent = project(columns, *parts)
        strips[chip] = hand_back(add(tok, 0, kept, swap_core(sent)), *chip)
        return strips[chip]

    block, columns = barrier((block, columns))
    row1, side0 = shift_z(block), swap_y(block)
    home = send_home((0, 0), block)
    row1, side0, strips[0, 0] = barrier((row1, side0, home))
    row2, side1 = shift_z(row1), swap_y(row1)
    home = send_home((0, 1), side0), send_home((1, 0), row1)
    row2, side1, strips[0, 1], strips[1, 0] = barrier((row2, side1, *home))
    row3, side2 = shift_z(row2), swap_y(row2)
    home = send_home((1, 1), side1), send_home((2, 0), row2)
    row3, side2, strips[1, 1], strips[2, 0] = barrier((row3, side2, *home))
    low, high = halves(row3)[0], halves(side2)[1]
    low, high = barrier((low, high))
    low, high = swap_y(low), shift_z(high)
    home = send_home((2, 1), side2), send_home((3, 0), row3)
    low, high, strips[2, 1], strips[3, 0] = barrier((low, high, *home))
    send_home((3, 1), low, high)
    attn, normed = normalise(up_chips, [strips[chip] for chip in CHIPS], norm_gain)

    def run(r, *blocks):
        return expert(r, where, k_own, k_other, blocks, weights)

    gate_proj, up_proj, down_proj, normed = barrier((gate_proj, up_proj, down_proj, normed))
    row1, side0 = shift_z(normed), swap_y(normed)
    over00 = swap_core(normed)
    weights = [load(w) for w in (gate_proj, up_proj, down_proj)]
    row1, side0, over00, *weights = barrier((row1, side0, over00, *weights))
    row2, side1 = shift_z(row1), swap_y(row1)
    over01, over10 = swap_core(side0), swap_core(row1)
    out0 = run(0, normed, side0, over00, over01)
    row2, side1, over10, *out0 = barrier((row2, side1, over10, *out0))
    row3, side2 = shift_z(row2), swap_y(row2)
    over11, over20 = swap_core(side1), swap_core(row2)
    mate0 = swap_core(out0[1])
    out1 = run(1, row1, side1, over10, over11)
    row3, side2, over20, mate0, *out1 = barrier((row3, side2, over20, mate0, *out1))
    side3 = shift_z(side2)
    over21, over30 = swap_core(side2), swap_core(row3)
    mate1 = swap_core(out1[1])
    far1 = add(tok, tok, out1[0], mate1)
    over21, over30, far1 = barrier((over21, over30, far1))
    side1 = swap_y(far1)
    out2 = run(2, row2, side2, over20, over21)
    side3, side1, *out2 = barrier((side3, side1, *out2))
    over31 = swap_core(side3)
    mate2 = swap_core(out2[1])
    far2 = add(tok, tok, out2[0], mate2)
    acc = add(tok, 0, out1[0], mate1, side1)
    over31, far2, acc = barrier((over31, far2, acc))
    acc, side2 = shift_z(acc), swap_y(far2)
    out3 = run(3, row3, side3, over30, over31)
    acc, side2, *out3 = barrier((acc, side2, *out3))
    acc = add(tok, 0, acc, out2[0], mate2, side2)
    far0 = add(tok, tok, out0[0], mate0)
    mate3 = swap_core(out3[1])
    far3 = add(tok, tok, out3[0], mate3)
    acc, far3, far0 = barrier((acc, far3, far0))
    acc, side3 = shift_z(acc), swap_y(far3)
    acc, side3 = barrier((acc, side3))
    acc = add(tok, 0, acc, out3[0], mate3, side3)
    acc, far0 = barrier((acc, far0))
    acc, side0 = shift_z(acc), swap_y(far0)
    return add(tok, 0, attn, acc, out0[0], mate0, side0)


def solution(mesh):
    names = ("expert",)
    body = local
    shape = mesh.shape
    if shape["expert"] == NZ * NY * NC and shape["tensor"] == 1:
        groups = shape["groups"]
        mesh = Mesh(mesh.devices.reshape(groups, NZ, NY, NC, 1), ("groups", "z", "y", "core", "tensor"))
        names = ("z", "y", "core")
        body = boxed
    every = ("groups",) + names
    in_specs = (
        P(every, "tensor", None),
        P(every, None),
        P("tensor", names, None),
        P("tensor", names),
        P(),
        P(names, None, "tensor"),
        P(names, None, "tensor"),
        P(names, "tensor", None),
        P(every + ("tensor",), None),
        P(every + ("tensor",), None),
    )
    out_specs = P(every + ("tensor",), None)
    return jax.shard_map(body, mesh=mesh, in_specs=in_specs, out_specs=out_specs, check_vma=False)
```

```python
import jax
import jax.numpy as jnp
from jax import lax
from jax.experimental import pallas as pl
from jax.experimental.pallas import tpu as pltpu
from jax.sharding import Mesh, PartitionSpec as P

LAT = 256
VD = 128
TOP = 8
NZ, NY, NC = 4, 2, 2


score_scale = 0.0722


def local(
    queries,
    kv_latent,
    value_up,
    out_proj,
    norm_gain,
    gate_proj,
    up_proj,
    down_proj,
    routes,
    route_weights,
):
    tok, heads, width = queries.shape
    query_place = lax.axis_index("expert") * tok + jnp.arange(tok)
    piece = lax.all_gather(kv_latent, "expert", axis=0, tiled=True)
    running = jnp.full((tok, heads), -1e30, jnp.float32)
    count = piece.shape[0]
    scores = (
        jnp.einsum("shc,tc->sht", queries, piece, preferred_element_type=jnp.float32) * score_scale
    )
    key_place = jnp.arange(count)
    allowed = (query_place[:, None] >= key_place[None, :])[:, None, :]
    scores = jnp.where(allowed, scores, -1e30)
    newer = jnp.maximum(running, jnp.max(scores, axis=-1))
    expo = jnp.where(allowed, jnp.exp(scores - newer[..., None]), 0.0)
    total = jnp.sum(expo, axis=-1)
    update = jnp.einsum(
        "sht,tc->shc", expo.astype(jnp.bfloat16), piece[:, :LAT], preferred_element_type=jnp.float32
    )
    running, total, acc = (newer, total, update)
    latent_out = (acc / total[..., None]).astype(jnp.bfloat16)
    lifted = jnp.einsum(
        "shc,hcv->shv",
        latent_out,
        lax.all_gather(value_up, "expert", axis=1, tiled=True),
        preferred_element_type=jnp.float32,
    )
    flat_heads = lifted.astype(jnp.bfloat16).reshape(tok, heads * VD)
    partial_cols = jnp.dot(
        lax.all_gather(flat_heads, "expert", axis=0, tiled=True),
        out_proj,
        preferred_element_type=jnp.float32,
    )
    wide_rows = lax.all_to_all(
        partial_cols.astype(jnp.bfloat16), "expert", split_axis=0, concat_axis=1, tiled=True
    ).astype(partial_cols.dtype)
    attn = lax.psum_scatter(
        wide_rows.astype(jnp.bfloat16), "tensor", scatter_dimension=0, tiled=True
    )
    attn32 = attn.astype(jnp.float32)
    scale = lax.rsqrt(jnp.mean(attn32 * attn32, axis=-1, keepdims=True) + 1e-06)
    normed = (attn32 * scale * norm_gain).astype(jnp.bfloat16)
    rows = routes.shape[0]
    experts = lax.axis_size("expert") * gate_proj.shape[0]
    capacity = min(rows, max(2, 5 * rows * TOP // (4 * experts)))
    width_d = normed.shape[1]
    flat_routes = routes.reshape(-1)
    onehot = (flat_routes[:, None] == jnp.arange(experts)[None, :]).astype(jnp.int32)
    before = jnp.cumsum(onehot, axis=0) - onehot
    slot = jnp.sum(before * onehot, axis=1).reshape(rows, TOP)
    target = routes * capacity + slot
    slot_ids = jnp.arange(experts * capacity)
    placing = jnp.sum(
        (target[None, :, :] == slot_ids[:, None, None]).astype(jnp.int32), axis=2
    ).astype(jnp.bfloat16)
    outbound = jnp.dot(placing, normed, preferred_element_type=jnp.float32).astype(jnp.bfloat16)
    arrived = lax.all_to_all(
        outbound.reshape(experts, capacity, width_d),
        "expert",
        split_axis=0,
        concat_axis=0,
        tiled=True,
    )
    both_halves = lax.all_gather(arrived, "tensor", axis=0, tiled=True).reshape(-1, width_d)
    gate = jnp.dot(both_halves, gate_proj[0], preferred_element_type=jnp.float32)
    upper = jnp.dot(both_halves, up_proj[0], preferred_element_type=jnp.float32)
    hidden = (jax.nn.silu(gate) * upper).astype(jnp.bfloat16)
    down_terms = jnp.dot(hidden, down_proj[0], preferred_element_type=jnp.float32)
    expert_out = lax.psum_scatter(
        down_terms.astype(jnp.bfloat16), "tensor", scatter_dimension=0, tiled=True
    )
    back = lax.all_to_all(
        expert_out.reshape(experts, capacity, width_d),
        "expert",
        split_axis=0,
        concat_axis=0,
        tiled=True,
    )
    picked = back.reshape(-1, width_d)[target]
    mixed = jnp.sum(route_weights[:, :, None] * picked.astype(jnp.float32), axis=1)
    return (attn32 + mixed).astype(jnp.bfloat16)


CHIPS = [(r, b) for r in range(NZ) for b in range(NY)]
NT = (((1,), (1,)), ((), ()))
F32, B16 = jnp.float32, jnp.bfloat16
WHOLE = pl.BlockSpec(memory_space=pltpu.VMEM)
barrier = lax.optimization_barrier


def shift_z(value, by=1):
    return lax.ppermute(value, "z", [(i, (i + by) % NZ) for i in range(NZ)])


def swap_y(value):
    return lax.ppermute(value, "y", [(0, 1), (1, 0)])


def swap_core(value):
    return lax.ppermute(value, "core", [(0, 1), (1, 0)])


def hand_back(value, r, b):
    if r == 0 and b == 0:
        return value
    pairs = [
        (z * NY + y, ((z - r) % NZ) * NY + (y ^ b)) for z in range(NZ) for y in range(NY)
    ]
    return lax.ppermute(value, ("z", "y"), pairs)


def call(kernel, outs, scratch, limit, flops, name, *args):
    size = sum(a.size * a.dtype.itemsize for a in args)
    return pl.pallas_call(
        kernel,
        in_specs=[
            pl.BlockSpec(memory_space=pltpu.SMEM) if a.ndim == 1 else WHOLE for a in args
        ],
        out_specs=[WHOLE] * len(outs),
        out_shape=[
            jax.ShapeDtypeStruct(o, B16) if isinstance(o, tuple) else o for o in outs
        ],
        scratch_shapes=scratch,
        compiler_params=pltpu.CompilerParams(vmem_limit_bytes=limit << 20),
        cost_estimate=pl.CostEstimate(flops=flops, bytes_accessed=size, transcendentals=0),
        name=name,
    )(*args)


def prepare(where, kv_latent, routes, route_weights, value_up, experts):
    tok, width = kv_latent.shape
    heads, part, _ = value_up.shape
    half = heads // NC

    def kernel(where, kv, routed, weight, v, out, own, send):
        dense = jnp.zeros((experts, tok), F32)
        number = lax.broadcasted_iota(jnp.int32, (experts, tok), 0)
        for k in range(TOP):
            dense = dense + jnp.where(routed[k : k + 1] == number, weight[k : k + 1], 0.0)
        high = dense.astype(B16)
        low = (dense - high.astype(F32)).astype(B16)
        same = lax.broadcasted_iota(jnp.int32, (tok, tok), 0) == lax.broadcasted_iota(
            jnp.int32, (tok, tok), 1
        )
        eye = jnp.where(same, 1.0, 0.0).astype(B16)
        out[:, :width] = kv[...]
        for n, term in enumerate((high, low)):
            at = width + n * experts
            out[:, at : at + experts] = lax.dot_general(
                eye, term, NT, preferred_element_type=F32
            ).astype(B16)
        for at, ref in ((where[0], own), (1 - where[0], send)):
            ref[...] = v[pl.ds(pl.multiple_of(at * half, half), half)]

    return call(
        kernel,
        [(tok, width + 2 * experts)] + [(half, part, VD)] * 2,
        [],
        4,
        1 << 20,
        "prepare",
        where,
        kv_latent,
        routes.T,
        route_weights.T,
        value_up,
    )


def split_heads(where, queries):
    tok, heads, width = queries.shape
    half = heads // NC

    def kernel(where, q, own, send):
        for at, out in ((where[0], own), (1 - where[0], send)):
            first = pl.multiple_of(at * half, half)
            out[...] = jnp.swapaxes(q[:, pl.ds(first, half), :], 0, 1)

    shapes = [(half, tok, width)] * 2
    return call(kernel, shapes, [], 16, 1 << 16, "split_heads", where, queries)


def join_cores(where, own, other):
    heads, part, width = own.shape

    def kernel(where, a, b, out):
        out[:, pl.ds(pl.multiple_of(where[0] * part, part), part), :] = a[...]
        out[:, pl.ds(pl.multiple_of((1 - where[0]) * part, part), part), :] = b[...]

    return call(
        kernel, [(heads, 2 * part, width)], [], 4, 1 << 10, "join_cores", where, own, other
    )[0]


def stack_rows(blocks):
    rows, width = blocks[0].shape

    def kernel(*refs):
        for n, ref in enumerate(refs[:-1]):
            refs[-1][n * rows : (n + 1) * rows] = ref[...]

    return call(kernel, [(rows * len(blocks), width)], [], 2, 1 << 16, "stack_rows", *blocks)[0]


def attend(which, bases, q_own, q_other, k_own, k_other):
    heads, tok, width = q_own.shape
    heads = heads // 2
    half = k_own.shape[0]
    rows = 2 * tok
    hb, sub = 8, 2
    turn = score_scale * 1.4426950408889634

    def kernel(base, qo, qx, ko, kx, out, bias):
        step = lax.broadcasted_iota(jnp.int32, (tok, tok), 0) - lax.broadcasted_iota(
            jnp.int32, (tok, tok), 1
        )
        for d in range(2):
            for n in range(2 * half // tok):
                seen = jnp.where(step + (base[d] - base[2 + n]) >= 0, 0.0, -1e30)
                for j in range(sub):
                    at = j * rows + d * tok
                    bias[at : at + tok, n * tok : (n + 1) * tok] = seen
        first = which * heads

        def body(turns, _):
            at = turns * hb
            for g in range(0, hb, sub):
                q = jnp.concatenate(
                    [ref[first + at + j] for j in range(g, g + sub) for ref in (qo, qx)], axis=0
                )
                s0 = lax.dot_general(q, ko[:, :width], NT, preferred_element_type=F32)
                s1 = lax.dot_general(q, kx[:, :width], NT, preferred_element_type=F32)
                s0 = s0 + bias[:, :half]
                s1 = s1 + bias[:, half:]
                top = jnp.maximum(
                    jnp.max(s0, axis=-1, keepdims=True), jnp.max(s1, axis=-1, keepdims=True)
                )
                p0 = jnp.exp2((s0 - top) * turn)
                p1 = jnp.exp2((s1 - top) * turn)
                total = jnp.sum(p0, axis=-1, keepdims=True) + jnp.sum(p1, axis=-1, keepdims=True)
                acc = jnp.dot(p0.astype(B16), ko[:, :LAT], preferred_element_type=F32)
                acc = acc + jnp.dot(p1.astype(B16), kx[:, :LAT], preferred_element_type=F32)
                latent = (acc / total).astype(B16)
                for j in range(sub):
                    out[at + g + j] = latent[j * rows : (j + 1) * rows]
            return 0

        lax.fori_loop(0, heads // hb, body, 0)

    return call(
        kernel,
        [(heads, rows, LAT)],
        [pltpu.VMEM((sub * rows, 2 * half), F32)],
        16,
        2 * heads * rows * 2 * half * (width + LAT),
        "attend",
        bases,
        q_own,
        q_other,
        k_own,
        k_other,
    )[0]


def raise_values(chips, latents, pieces):
    heads, rows, _ = latents[0].shape
    part = pieces[0].shape[1]
    n = len(latents)

    def kernel(chip, *refs):
        lat, parts, out, lift = refs[:n], refs[n:-2], refs[-2], refs[-1]
        for at, ref in enumerate(parts):
            lift[:, pl.ds(pl.multiple_of(chip[at] * part, part), part), :] = ref[...]
        for j in range(n * heads):
            out[:, j * VD : (j + 1) * VD] = jnp.dot(
                lat[j // heads][j % heads], lift[j], preferred_element_type=F32
            ).astype(B16)

    return call(
        kernel,
        [(rows, n * heads * VD)],
        [pltpu.VMEM((n * heads, LAT, VD), B16)],
        8,
        2 * n * heads * rows * LAT * VD,
        "raise_values",
        chips,
        *latents,
        *pieces,
    )[0]


def split_proj(where, flat):
    cols, rows = flat.shape
    half = rows // NC

    def kernel(where, a, own, send):
        own[...] = a[:, pl.ds(pl.multiple_of(where[0] * half, half), half)]
        send[...] = a[:, pl.ds(pl.multiple_of((1 - where[0]) * half, half), half)]

    return call(kernel, [(cols, half)] * 2, [], 4, 1 << 16, "split_proj", where, flat)


def join_proj(where, own, other):
    cols, rows = own.shape

    def kernel(where, a, b, out):
        out[pl.ds(pl.multiple_of(where[0] * cols, 16), cols), :] = a[...]
        out[pl.ds(pl.multiple_of((1 - where[0]) * cols, 16), cols), :] = b[...]

    return call(kernel, [(2 * cols, rows)], [], 4, 1 << 16, "join_proj", where, own, other)[0]


def halves(first, second):
    rows = first.shape[0] // 2

    def kernel(a, b, low, high):
        low[...] = a[:rows]
        high[...] = b[rows:]

    return call(kernel, [(rows, first.shape[1])] * 2, [], 2, 1 << 16, "halves", first, second)


def project(columns, *parts):
    rows = sum(part.shape[0] for part in parts)
    cols, depth = columns.shape
    tok = rows // 2

    def kernel(b, *refs):
        keep, send = refs[-2:]
        piece = jnp.concatenate([ref[...] for ref in refs[:-2]], axis=0)
        part = lax.dot_general(piece, b[...], NT, preferred_element_type=F32)
        keep[...] = part[:tok]
        send[...] = part[tok:].astype(B16)

    return call(
        kernel,
        [jax.ShapeDtypeStruct((tok, cols), F32), (tok, cols)],
        [],
        6,
        2 * rows * depth * cols,
        "project",
        columns,
        *parts,
    )


def add(rows, at, *terms):
    def kernel(*refs):
        total = 0.0
        for ref in refs[:-1]:
            block = ref[...] if ref.shape[0] == rows else ref[at : at + rows]
            total = total + block.astype(F32)
        refs[-1][...] = total.astype(B16)

    shape = (rows, terms[0].shape[1])
    return call(kernel, [shape], [], 4, rows * shape[1], "add", *terms)[0]


def normalise(chips, strips, norm_gain):
    tok, cols = strips[0].shape
    wide = len(CHIPS) * cols

    def kernel(chip, gain, *refs):
        parts, attn, normed, stage, full = refs[: len(CHIPS)], *refs[-4:]
        for n, ref in enumerate(parts):
            stage[chip[n]] = ref[...].astype(F32)
        for n in range(len(CHIPS)):
            full[:, n * cols : (n + 1) * cols] = stage[n]
        value = full[...]
        attn[...] = value.astype(B16)
        scale = lax.rsqrt(jnp.mean(value * value, axis=-1, keepdims=True) + 1e-06)
        normed[...] = (value * scale * gain[...]).astype(B16)

    return call(
        kernel,
        [(tok, wide)] * 2,
        [pltpu.VMEM((len(CHIPS), tok, cols), F32), pltpu.VMEM((tok, wide), F32)],
        8,
        1 << 20,
        "normalise",
        chips,
        norm_gain.reshape(1, -1),
        *strips,
    )


def load(weight):
    def kernel(source, out, sem):
        copy = pltpu.make_async_copy(source, out, sem)
        copy.start()
        copy.wait()

    return pl.pallas_call(
        kernel,
        in_specs=[pl.BlockSpec(memory_space=pltpu.HBM)],
        out_specs=WHOLE,
        out_shape=jax.ShapeDtypeStruct(weight.shape, weight.dtype),
        scratch_shapes=[pltpu.SemaphoreType.DMA],
        compiler_params=pltpu.CompilerParams(vmem_limit_bytes=2 << 20),
        cost_estimate=pl.CostEstimate(flops=0, bytes_accessed=weight.size * 2, transcendentals=0),
        name="load",
    )(weight)


def expert(r, where, k_own, blocks, weights):
    tok, width = blocks[0].shape
    units = weights[0].shape[2]
    fb, nb = 256, 512
    n = len(blocks)
    rows = n * tok
    dense = k_own.shape[1]
    experts = len(CHIPS) * NC

    def kernel(where, ko, *refs):
        mats, refs = refs[: 3 * NC], refs[3 * NC :]
        ins, outs, x, hidden, share = refs[:n], refs[n : 2 * n], *refs[2 * n :]
        lane = lax.broadcasted_iota(jnp.int32, (tok, 2 * experts), 1)
        for b in range(n):
            at = (b * NZ + r) * tok
            table = ko[at : at + tok, dense - 2 * experts :].astype(F32)
            for e in range(NC):
                number = where[1 + e]
                mine = (lane == number) | (lane == number + experts)
                share[b * tok : (b + 1) * tok, e : e + 1] = jnp.sum(
                    jnp.where(mine, table, 0.0), axis=-1, keepdims=True
                )
            x[b * tok : (b + 1) * tok] = ins[b][...]
        for e in range(NC):
            gate_w, up_w = mats[3 * e], mats[3 * e + 1]
            for f in range(0, units, fb):
                gate = jnp.dot(x[...], gate_w[0, :, f : f + fb], preferred_element_type=F32)
                upper = jnp.dot(x[...], up_w[0, :, f : f + fb], preferred_element_type=F32)
                hidden[e, :, f : f + fb] = (jax.nn.silu(gate) * upper).astype(B16)
        for c in range(0, width, nb):
            out = 0.0
            for e in range(NC):
                down = jnp.dot(
                    hidden[e], mats[3 * e + 2][0, :, c : c + nb], preferred_element_type=F32
                )
                out = out + down * share[:, e : e + 1]
            out = out.astype(B16)
            for b in range(n):
                outs[b][:, c : c + nb] = out[b * tok : (b + 1) * tok]

    return call(
        kernel,
        [(tok, width)] * n,
        [
            pltpu.VMEM((rows, width), B16),
            pltpu.VMEM((NC, rows, units), B16),
            pltpu.VMEM((rows, NC), F32),
        ],
        6,
        12 * rows * width * units,
        "expert",
        where,
        k_own,
        *weights,
        *blocks,
    )


def boxed(
    queries,
    kv_latent,
    value_up,
    out_proj,
    norm_gain,
    gate_proj,
    up_proj,
    down_proj,
    routes,
    route_weights,
):
    tok, heads, width = queries.shape
    z, y, core = (lax.axis_index(name) for name in ("z", "y", "core"))
    experts = NZ * NY * NC
    place = (z * NY + y) * NC + core
    where = jnp.stack([core, place, place ^ 1]).astype(jnp.int32)
    up_chips = jnp.stack([((z + r) % NZ) * NY + (y ^ b) for r, b in CHIPS])
    down_chips = jnp.stack([((z - r) % NZ) * NY + (y ^ b) for r, b in CHIPS])
    key_chips = jnp.stack([((z - r) % NZ) * NY + (y ^ b) for b in range(NY) for r in range(NZ)])
    bases = [jnp.stack([place, place ^ 1]), key_chips * NC + core, key_chips * NC + (core ^ 1)]
    bases = (jnp.concatenate(bases) * tok).astype(jnp.int32)
    where, up_chips, down_chips, bases, kv_latent = barrier(
        (where, up_chips, down_chips, bases, kv_latent)
    )

    pack, lift_own, lift_send = prepare(
        where, kv_latent, routes, route_weights, value_up, experts
    )
    queries, pack = barrier((queries, pack))
    keys = [pack] + [shift_z(pack, r) for r in range(1, NZ)]
    lift = join_cores(where, lift_own, swap_core(lift_send))
    queries, lift = barrier((queries, lift))
    up1, side0 = shift_z(lift), swap_y(lift)
    q_own, q_send = split_heads(where, queries)
    *keys, up1, side0, q_own, q_send = barrier((*keys, up1, side0, q_own, q_send))

    column = stack_rows(keys)
    beside = swap_y(column)
    up2, side1 = shift_z(up1), swap_y(up1)
    q_other = swap_core(q_send)
    beside, up2, side1, q_other = barrier((beside, up2, side1, q_other))
    k_own = stack_rows([column, beside])
    k_other = swap_core(k_own)
    up3, side2 = shift_z(up2), swap_y(up2)
    latent0 = attend(0, bases, q_own, q_other, k_own, k_other)
    up3, side2, latent0, q_own = barrier((up3, side2, latent0, q_own))
    side3 = swap_y(up3)
    latent1 = attend(1, bases, q_own, q_other, k_own, k_other)
    side3, latent1 = barrier((side3, latent1))
    lifts = (lift, side0, up1, side1, up2, side2, up3, side3)
    block = raise_values(down_chips, (latent0, latent1), lifts)

    strips = {}

    def send_home(chip, *parts):
        kept, sent = project(columns, *parts)
        strips[chip] = add(tok, 0, kept, swap_core(sent))
        return strips[chip]

    block, out_proj, gate_proj, up_proj, down_proj = barrier(
        (block, out_proj, gate_proj, up_proj, down_proj)
    )
    row1, side0 = shift_z(block), swap_y(block)
    gate_other = swap_core(gate_proj)
    proj_own, proj_send = split_proj(where, out_proj.T)
    columns = join_proj(where, proj_own, swap_core(proj_send))
    home = send_home((0, 0), block)
    row1, side0, strips[0, 0], gate_other, up_proj = barrier(
        (row1, side0, home, gate_other, up_proj)
    )
    row2, side1 = shift_z(row1), swap_y(row1)
    up_other = swap_core(up_proj)
    home = send_home((0, 1), side0), send_home((1, 0), row1)
    row2, side1, strips[0, 1], strips[1, 0], up_other, down_proj = barrier(
        (row2, side1, *home, up_other, down_proj)
    )
    row3, side2 = shift_z(row2), swap_y(row2)
    down_other = swap_core(down_proj)
    home = send_home((1, 1), side1), send_home((2, 0), row2)
    row3, side2, strips[1, 1], strips[2, 0], down_other = barrier(
        (row3, side2, *home, down_other)
    )
    low, high = halves(row3, side2)
    low, high = barrier((low, high))
    low, high = swap_y(low), shift_z(high)
    home = send_home((2, 1), side2), send_home((3, 0), row3)
    low, high, strips[2, 1], strips[3, 0] = barrier((low, high, *home))
    send_home((3, 1), low, high)
    for chip in CHIPS:
        strips[chip] = hand_back(strips[chip], *chip)
    attn, normed = normalise(up_chips, [strips[chip] for chip in CHIPS], norm_gain)

    gate_proj, up_proj, down_proj, normed = barrier((gate_proj, up_proj, down_proj, normed))
    row1, side0 = shift_z(normed), swap_y(normed)
    weights = [load(w) for w in (gate_proj, up_proj, down_proj)]
    weights += [gate_other, up_other, down_other]
    row1, side0, *weights = barrier((row1, side0, *weights))

    def run(r, *blocks):
        return expert(r, where, k_own, blocks, weights)

    row2, side1 = shift_z(row1), swap_y(row1)
    near0, far0 = run(0, normed, side0)
    row2, side1, near0, far0 = barrier((row2, side1, near0, far0))
    row3, side2 = shift_z(row2), swap_y(row2)
    near1, far1 = run(1, row1, side1)
    row3, side2, near1, far1 = barrier((row3, side2, near1, far1))
    side3, side1 = shift_z(side2), swap_y(far1)
    near2, far2 = run(2, row2, side2)
    side3, side1, near2, far2 = barrier((side3, side1, near2, far2))
    acc, side2 = shift_z(add(tok, 0, near1, side1)), swap_y(far2)
    near3, far3 = run(3, row3, side3)
    acc, side2, near3, far3 = barrier((acc, side2, near3, far3))
    acc, side3 = shift_z(add(tok, 0, acc, near2, side2)), swap_y(far3)
    acc, side3, far0 = barrier((acc, side3, far0))
    acc, side0 = shift_z(add(tok, 0, acc, near3, side3)), swap_y(far0)
    return add(tok, 0, attn, acc, near0, side0)


def solution(mesh):
    names = ("expert",)
    body = local
    shape = mesh.shape
    if shape["expert"] == NZ * NY * NC and shape["tensor"] == 1:
        groups = shape["groups"]
        mesh = Mesh(mesh.devices.reshape(groups, NZ, NY, NC, 1), ("groups", "z", "y", "core", "tensor"))
        names = ("z", "y", "core")
        body = boxed
    every = ("groups",) + names
    in_specs = (
        P(every, "tensor", None),
        P(every, None),
        P("tensor", names, None),
        P("tensor", names),
        P(),
        P(names, None, "tensor"),
        P(names, None, "tensor"),
        P(names, "tensor", None),
        P(every + ("tensor",), None),
        P(every + ("tensor",), None),
    )
    out_specs = P(every + ("tensor",), None)
    return jax.shard_map(body, mesh=mesh, in_specs=in_specs, out_specs=out_specs, check_vma=False)
```

```python
import jax
import jax.numpy as jnp
from jax import lax
from jax.experimental import pallas as pl
from jax.experimental.pallas import tpu as pltpu
from jax.sharding import Mesh, PartitionSpec as P

LAT = 256
VD = 128
TOP = 8
NZ, NY, NC = 4, 2, 2


score_scale = 0.0722


def local(
    queries,
    kv_latent,
    value_up,
    out_proj,
    norm_gain,
    gate_proj,
    up_proj,
    down_proj,
    routes,
    route_weights,
):
    tok, heads, width = queries.shape
    query_place = lax.axis_index("expert") * tok + jnp.arange(tok)
    piece = lax.all_gather(kv_latent, "expert", axis=0, tiled=True)
    running = jnp.full((tok, heads), -1e30, jnp.float32)
    count = piece.shape[0]
    scores = (
        jnp.einsum("shc,tc->sht", queries, piece, preferred_element_type=jnp.float32) * score_scale
    )
    key_place = jnp.arange(count)
    allowed = (query_place[:, None] >= key_place[None, :])[:, None, :]
    scores = jnp.where(allowed, scores, -1e30)
    newer = jnp.maximum(running, jnp.max(scores, axis=-1))
    expo = jnp.where(allowed, jnp.exp(scores - newer[..., None]), 0.0)
    total = jnp.sum(expo, axis=-1)
    update = jnp.einsum(
        "sht,tc->shc", expo.astype(jnp.bfloat16), piece[:, :LAT], preferred_element_type=jnp.float32
    )
    running, total, acc = (newer, total, update)
    latent_out = (acc / total[..., None]).astype(jnp.bfloat16)
    lifted = jnp.einsum(
        "shc,hcv->shv",
        latent_out,
        lax.all_gather(value_up, "expert", axis=1, tiled=True),
        preferred_element_type=jnp.float32,
    )
    flat_heads = lifted.astype(jnp.bfloat16).reshape(tok, heads * VD)
    partial_cols = jnp.dot(
        lax.all_gather(flat_heads, "expert", axis=0, tiled=True),
        out_proj,
        preferred_element_type=jnp.float32,
    )
    wide_rows = lax.all_to_all(
        partial_cols.astype(jnp.bfloat16), "expert", split_axis=0, concat_axis=1, tiled=True
    ).astype(partial_cols.dtype)
    attn = lax.psum_scatter(
        wide_rows.astype(jnp.bfloat16), "tensor", scatter_dimension=0, tiled=True
    )
    attn32 = attn.astype(jnp.float32)
    scale = lax.rsqrt(jnp.mean(attn32 * attn32, axis=-1, keepdims=True) + 1e-06)
    normed = (attn32 * scale * norm_gain).astype(jnp.bfloat16)
    rows = routes.shape[0]
    experts = lax.axis_size("expert") * gate_proj.shape[0]
    capacity = min(rows, max(2, 5 * rows * TOP // (4 * experts)))
    width_d = normed.shape[1]
    flat_routes = routes.reshape(-1)
    onehot = (flat_routes[:, None] == jnp.arange(experts)[None, :]).astype(jnp.int32)
    before = jnp.cumsum(onehot, axis=0) - onehot
    slot = jnp.sum(before * onehot, axis=1).reshape(rows, TOP)
    target = routes * capacity + slot
    slot_ids = jnp.arange(experts * capacity)
    placing = jnp.sum(
        (target[None, :, :] == slot_ids[:, None, None]).astype(jnp.int32), axis=2
    ).astype(jnp.bfloat16)
    outbound = jnp.dot(placing, normed, preferred_element_type=jnp.float32).astype(jnp.bfloat16)
    arrived = lax.all_to_all(
        outbound.reshape(experts, capacity, width_d),
        "expert",
        split_axis=0,
        concat_axis=0,
        tiled=True,
    )
    both_halves = lax.all_gather(arrived, "tensor", axis=0, tiled=True).reshape(-1, width_d)
    gate = jnp.dot(both_halves, gate_proj[0], preferred_element_type=jnp.float32)
    upper = jnp.dot(both_halves, up_proj[0], preferred_element_type=jnp.float32)
    hidden = (jax.nn.silu(gate) * upper).astype(jnp.bfloat16)
    down_terms = jnp.dot(hidden, down_proj[0], preferred_element_type=jnp.float32)
    expert_out = lax.psum_scatter(
        down_terms.astype(jnp.bfloat16), "tensor", scatter_dimension=0, tiled=True
    )
    back = lax.all_to_all(
        expert_out.reshape(experts, capacity, width_d),
        "expert",
        split_axis=0,
        concat_axis=0,
        tiled=True,
    )
    picked = back.reshape(-1, width_d)[target]
    mixed = jnp.sum(route_weights[:, :, None] * picked.astype(jnp.float32), axis=1)
    return (attn32 + mixed).astype(jnp.bfloat16)


CHIPS = [(r, b) for r in range(NZ) for b in range(NY)]
NT = (((1,), (1,)), ((), ()))
F32, B16 = jnp.float32, jnp.bfloat16
WHOLE = pl.BlockSpec(memory_space=pltpu.VMEM)
barrier = lax.optimization_barrier


def fold(at):
    return at ^ (at >> 1)


def step_z(z, by):
    return fold((fold(z) + by) % NZ)


def shift_z(value, by=1):
    return lax.ppermute(value, "z", [(z, step_z(z, by)) for z in range(NZ)])


def swap_y(value):
    return lax.ppermute(value, "y", [(0, 1), (1, 0)])


def swap_core(value):
    return lax.ppermute(value, "core", [(0, 1), (1, 0)])


def hand_back(value, r, b):
    if r == 0 and b == 0:
        return value
    pairs = [
        (z * NY + y, step_z(z, -r) * NY + (y ^ b)) for z in range(NZ) for y in range(NY)
    ]
    return lax.ppermute(value, ("z", "y"), pairs)


def call(kernel, outs, scratch, limit, flops, name, *args):
    size = sum(a.size * a.dtype.itemsize for a in args)
    return pl.pallas_call(
        kernel,
        in_specs=[
            pl.BlockSpec(memory_space=pltpu.SMEM) if a.ndim == 1 else WHOLE for a in args
        ],
        out_specs=[WHOLE] * len(outs),
        out_shape=[
            jax.ShapeDtypeStruct(o, B16) if isinstance(o, tuple) else o for o in outs
        ],
        scratch_shapes=scratch,
        compiler_params=pltpu.CompilerParams(vmem_limit_bytes=limit << 20),
        cost_estimate=pl.CostEstimate(flops=flops, bytes_accessed=size, transcendentals=0),
        name=name,
    )(*args)


def prepare(where, kv_latent, routes, route_weights, value_up, experts):
    tok, width = kv_latent.shape
    heads, part, _ = value_up.shape
    half = heads // NC

    def kernel(where, kv, routed, weight, v, out, own, send):
        dense = jnp.zeros((experts, tok), F32)
        number = lax.broadcasted_iota(jnp.int32, (experts, tok), 0)
        for k in range(TOP):
            dense = dense + jnp.where(routed[k : k + 1] == number, weight[k : k + 1], 0.0)
        high = dense.astype(B16)
        low = (dense - high.astype(F32)).astype(B16)
        same = lax.broadcasted_iota(jnp.int32, (tok, tok), 0) == lax.broadcasted_iota(
            jnp.int32, (tok, tok), 1
        )
        eye = jnp.where(same, 1.0, 0.0).astype(B16)
        out[:, :width] = kv[...]
        for n, term in enumerate((high, low)):
            at = width + n * experts
            out[:, at : at + experts] = lax.dot_general(
                eye, term, NT, preferred_element_type=F32
            ).astype(B16)
        for at, ref in ((where[0], own), (1 - where[0], send)):
            ref[...] = v[pl.ds(pl.multiple_of(at * half, half), half)]

    return call(
        kernel,
        [(tok, width + 2 * experts)] + [(half, part, VD)] * 2,
        [],
        4,
        1 << 20,
        "prepare",
        where,
        kv_latent,
        routes.T,
        route_weights.T,
        value_up,
    )


def split_heads(where, queries):
    tok, heads, width = queries.shape
    half = heads // NC

    def kernel(where, q, own, send):
        for at, out in ((where[0], own), (1 - where[0], send)):
            first = pl.multiple_of(at * half, half)
            out[...] = jnp.swapaxes(q[:, pl.ds(first, half), :], 0, 1)

    shapes = [(half, tok, width)] * 2
    return call(kernel, shapes, [], 16, 1 << 16, "split_heads", where, queries)


def join_cores(where, own, other):
    heads, part, width = own.shape

    def kernel(where, a, b, out):
        out[:, pl.ds(pl.multiple_of(where[0] * part, part), part), :] = a[...]
        out[:, pl.ds(pl.multiple_of((1 - where[0]) * part, part), part), :] = b[...]

    return call(
        kernel, [(heads, 2 * part, width)], [], 4, 1 << 10, "join_cores", where, own, other
    )[0]


def stack_rows(blocks):
    rows, width = blocks[0].shape

    def kernel(*refs):
        for n, ref in enumerate(refs[:-1]):
            refs[-1][n * rows : (n + 1) * rows] = ref[...]

    return call(kernel, [(rows * len(blocks), width)], [], 2, 1 << 16, "stack_rows", *blocks)[0]


def attend(which, bases, q_own, q_other, k_own, k_other):
    heads, tok, width = q_own.shape
    heads = heads // 2
    half = k_own.shape[0]
    rows = 2 * tok
    hb, sub = 8, 2
    turn = score_scale * 1.4426950408889634

    def kernel(base, qo, qx, ko, kx, out, bias):
        step = lax.broadcasted_iota(jnp.int32, (tok, tok), 0) - lax.broadcasted_iota(
            jnp.int32, (tok, tok), 1
        )
        for d in range(2):
            for n in range(2 * half // tok):
                seen = jnp.where(step + (base[d] - base[2 + n]) >= 0, 0.0, -1e30)
                for j in range(sub):
                    at = j * rows + d * tok
                    bias[at : at + tok, n * tok : (n + 1) * tok] = seen
        first = which * heads

        def body(turns, _):
            at = turns * hb
            for g in range(0, hb, sub):
                q = jnp.concatenate(
                    [ref[first + at + j] for j in range(g, g + sub) for ref in (qo, qx)], axis=0
                )
                s0 = lax.dot_general(q, ko[:, :width], NT, preferred_element_type=F32)
                s1 = lax.dot_general(q, kx[:, :width], NT, preferred_element_type=F32)
                s0 = s0 + bias[:, :half]
                s1 = s1 + bias[:, half:]
                top = jnp.maximum(
                    jnp.max(s0, axis=-1, keepdims=True), jnp.max(s1, axis=-1, keepdims=True)
                )
                p0 = jnp.exp2((s0 - top) * turn)
                p1 = jnp.exp2((s1 - top) * turn)
                total = jnp.sum(p0, axis=-1, keepdims=True) + jnp.sum(p1, axis=-1, keepdims=True)
                acc = jnp.dot(p0.astype(B16), ko[:, :LAT], preferred_element_type=F32)
                acc = acc + jnp.dot(p1.astype(B16), kx[:, :LAT], preferred_element_type=F32)
                latent = (acc / total).astype(B16)
                for j in range(sub):
                    out[at + g + j] = latent[j * rows : (j + 1) * rows]
            return 0

        lax.fori_loop(0, heads // hb, body, 0)

    return call(
        kernel,
        [(heads, rows, LAT)],
        [pltpu.VMEM((sub * rows, 2 * half), F32)],
        16,
        2 * heads * rows * 2 * half * (width + LAT),
        "attend",
        bases,
        q_own,
        q_other,
        k_own,
        k_other,
    )[0]


def raise_values(chips, latents, pieces):
    heads, rows, _ = latents[0].shape
    part = pieces[0].shape[1]
    n = len(latents)

    def kernel(chip, *refs):
        lat, parts, out, lift = refs[:n], refs[n:-2], refs[-2], refs[-1]
        for at, ref in enumerate(parts):
            lift[:, pl.ds(pl.multiple_of(chip[at] * part, part), part), :] = ref[...]
        for j in range(n * heads):
            out[:, j * VD : (j + 1) * VD] = jnp.dot(
                lat[j // heads][j % heads], lift[j], preferred_element_type=F32
            ).astype(B16)

    return call(
        kernel,
        [(rows, n * heads * VD)],
        [pltpu.VMEM((n * heads, LAT, VD), B16)],
        8,
        2 * n * heads * rows * LAT * VD,
        "raise_values",
        chips,
        *latents,
        *pieces,
    )[0]


def split_proj(where, flat):
    cols, rows = flat.shape
    half = rows // NC

    def kernel(where, a, own, send):
        own[...] = a[:, pl.ds(pl.multiple_of(where[0] * half, half), half)]
        send[...] = a[:, pl.ds(pl.multiple_of((1 - where[0]) * half, half), half)]

    return call(kernel, [(cols, half)] * 2, [], 4, 1 << 16, "split_proj", where, flat)


def join_proj(where, own, other):
    cols, rows = own.shape

    def kernel(where, a, b, out):
        out[pl.ds(pl.multiple_of(where[0] * cols, 16), cols), :] = a[...]
        out[pl.ds(pl.multiple_of((1 - where[0]) * cols, 16), cols), :] = b[...]

    return call(kernel, [(2 * cols, rows)], [], 4, 1 << 16, "join_proj", where, own, other)[0]


def halves(first, second):
    rows = first.shape[0] // 2

    def kernel(a, b, low, high):
        low[...] = a[:rows]
        high[...] = b[rows:]

    return call(kernel, [(rows, first.shape[1])] * 2, [], 2, 1 << 16, "halves", first, second)


def project(columns, *parts):
    rows = sum(part.shape[0] for part in parts)
    cols, depth = columns.shape
    tok = rows // 2

    def kernel(b, *refs):
        keep, send = refs[-2:]
        piece = jnp.concatenate([ref[...] for ref in refs[:-2]], axis=0)
        part = lax.dot_general(piece, b[...], NT, preferred_element_type=F32)
        keep[...] = part[:tok]
        send[...] = part[tok:].astype(B16)

    return call(
        kernel,
        [jax.ShapeDtypeStruct((tok, cols), F32), (tok, cols)],
        [],
        6,
        2 * rows * depth * cols,
        "project",
        columns,
        *parts,
    )


def add(rows, at, *terms):
    def kernel(*refs):
        total = 0.0
        for ref in refs[:-1]:
            block = ref[...] if ref.shape[0] == rows else ref[at : at + rows]
            total = total + block.astype(F32)
        refs[-1][...] = total.astype(B16)

    shape = (rows, terms[0].shape[1])
    return call(kernel, [shape], [], 4, rows * shape[1], "add", *terms)[0]


def normalise(chips, strips, norm_gain):
    tok, cols = strips[0].shape
    wide = len(CHIPS) * cols

    def kernel(chip, gain, *refs):
        parts, attn, normed, stage, full = refs[: len(CHIPS)], *refs[-4:]
        for n, ref in enumerate(parts):
            stage[chip[n]] = ref[...].astype(F32)
        for n in range(len(CHIPS)):
            full[:, n * cols : (n + 1) * cols] = stage[n]
        value = full[...]
        attn[...] = value.astype(B16)
        scale = lax.rsqrt(jnp.mean(value * value, axis=-1, keepdims=True) + 1e-06)
        normed[...] = (value * scale * gain[...]).astype(B16)

    return call(
        kernel,
        [(tok, wide)] * 2,
        [pltpu.VMEM((len(CHIPS), tok, cols), F32), pltpu.VMEM((tok, wide), F32)],
        8,
        1 << 20,
        "normalise",
        chips,
        norm_gain.reshape(1, -1),
        *strips,
    )


def load(weight):
    def kernel(source, out, sem):
        copy = pltpu.make_async_copy(source, out, sem)
        copy.start()
        copy.wait()

    return pl.pallas_call(
        kernel,
        in_specs=[pl.BlockSpec(memory_space=pltpu.HBM)],
        out_specs=WHOLE,
        out_shape=jax.ShapeDtypeStruct(weight.shape, weight.dtype),
        scratch_shapes=[pltpu.SemaphoreType.DMA],
        compiler_params=pltpu.CompilerParams(vmem_limit_bytes=2 << 20),
        cost_estimate=pl.CostEstimate(flops=0, bytes_accessed=weight.size * 2, transcendentals=0),
        name="load",
    )(weight)


def expert(r, where, k_own, blocks, weights):
    tok, width = blocks[0].shape
    units = weights[0].shape[2]
    fb, nb = 256, 512
    n = len(blocks)
    rows = n * tok
    dense = k_own.shape[1]
    experts = len(CHIPS) * NC

    def kernel(where, ko, *refs):
        mats, refs = refs[: 3 * NC], refs[3 * NC :]
        ins, outs, x, hidden, share = refs[:n], refs[n : 2 * n], *refs[2 * n :]
        lane = lax.broadcasted_iota(jnp.int32, (tok, 2 * experts), 1)
        for b in range(n):
            at = (b * NZ + r) * tok
            table = ko[at : at + tok, dense - 2 * experts :].astype(F32)
            for e in range(NC):
                number = where[1 + e]
                mine = (lane == number) | (lane == number + experts)
                share[b * tok : (b + 1) * tok, e : e + 1] = jnp.sum(
                    jnp.where(mine, table, 0.0), axis=-1, keepdims=True
                )
            x[b * tok : (b + 1) * tok] = ins[b][...]
        for e in range(NC):
            gate_w, up_w = mats[3 * e], mats[3 * e + 1]
            for f in range(0, units, fb):
                gate = jnp.dot(x[...], gate_w[0, :, f : f + fb], preferred_element_type=F32)
                upper = jnp.dot(x[...], up_w[0, :, f : f + fb], preferred_element_type=F32)
                hidden[e, :, f : f + fb] = (jax.nn.silu(gate) * upper).astype(B16)
        for c in range(0, width, nb):
            out = 0.0
            for e in range(NC):
                down = jnp.dot(
                    hidden[e], mats[3 * e + 2][0, :, c : c + nb], preferred_element_type=F32
                )
                out = out + down * share[:, e : e + 1]
            out = out.astype(B16)
            for b in range(n):
                outs[b][:, c : c + nb] = out[b * tok : (b + 1) * tok]

    return call(
        kernel,
        [(tok, width)] * n,
        [
            pltpu.VMEM((rows, width), B16),
            pltpu.VMEM((NC, rows, units), B16),
            pltpu.VMEM((rows, NC), F32),
        ],
        6,
        12 * rows * width * units,
        "expert",
        where,
        k_own,
        *weights,
        *blocks,
    )


def boxed(
    queries,
    kv_latent,
    value_up,
    out_proj,
    norm_gain,
    gate_proj,
    up_proj,
    down_proj,
    routes,
    route_weights,
):
    tok, heads, width = queries.shape
    z, y, core = (lax.axis_index(name) for name in ("z", "y", "core"))
    experts = NZ * NY * NC
    place = (z * NY + y) * NC + core
    where = jnp.stack([core, place, place ^ 1]).astype(jnp.int32)
    up_chips = jnp.stack([step_z(z, r) * NY + (y ^ b) for r, b in CHIPS])
    down_chips = jnp.stack([step_z(z, -r) * NY + (y ^ b) for r, b in CHIPS])
    key_chips = jnp.stack([step_z(z, -r) * NY + (y ^ b) for b in range(NY) for r in range(NZ)])
    bases = [jnp.stack([place, place ^ 1]), key_chips * NC + core, key_chips * NC + (core ^ 1)]
    bases = (jnp.concatenate(bases) * tok).astype(jnp.int32)
    where, up_chips, down_chips, bases, kv_latent = barrier(
        (where, up_chips, down_chips, bases, kv_latent)
    )

    pack, lift_own, lift_send = prepare(
        where, kv_latent, routes, route_weights, value_up, experts
    )
    queries, pack = barrier((queries, pack))
    keys = [pack] + [shift_z(pack, r) for r in range(1, NZ)]
    lift = join_cores(where, lift_own, swap_core(lift_send))
    queries, lift = barrier((queries, lift))
    up1, side0 = shift_z(lift), swap_y(lift)
    q_own, q_send = split_heads(where, queries)
    *keys, up1, side0, q_own, q_send = barrier((*keys, up1, side0, q_own, q_send))

    column = stack_rows(keys)
    beside = swap_y(column)
    up2 = shift_z(up1)
    q_other = swap_core(q_send)
    beside, up2, up1, side0, q_other = barrier((beside, up2, up1, side0, q_other))
    k_own = stack_rows([column, beside])
    k_other = swap_core(k_own)
    up3, side1 = shift_z(up2), swap_y(up1)
    latent0 = attend(0, bases, q_own, q_other, k_own, k_other)
    up3, side1, up2, side0, latent0, q_own = barrier((up3, side1, up2, side0, latent0, q_own))
    side2, side3 = swap_y(up2), shift_z(side0, -1)
    latent1 = attend(1, bases, q_own, q_other, k_own, k_other)
    side2, side3, latent1 = barrier((side2, side3, latent1))
    lifts = (lift, side0, up1, side1, up2, side2, up3, side3)
    block = raise_values(down_chips, (latent0, latent1), lifts)

    strips = {}

    def send_home(chip, *parts):
        kept, sent = project(columns, *parts)
        strips[chip] = add(tok, 0, kept, swap_core(sent))
        return strips[chip]

    block, out_proj, gate_proj, up_proj, down_proj = barrier(
        (block, out_proj, gate_proj, up_proj, down_proj)
    )
    row1, side0 = shift_z(block), swap_y(block)
    gate_other = swap_core(gate_proj)
    proj_own, proj_send = split_proj(where, out_proj.T)
    columns = join_proj(where, proj_own, swap_core(proj_send))
    home = send_home((0, 0), block)
    row1, side0, strips[0, 0], gate_other, up_proj = barrier(
        (row1, side0, home, gate_other, up_proj)
    )
    row2, side1 = shift_z(row1), swap_y(row1)
    up_other = swap_core(up_proj)
    home = send_home((0, 1), side0), send_home((1, 0), row1)
    row2, side1, strips[0, 1], strips[1, 0], up_other, down_proj = barrier(
        (row2, side1, *home, up_other, down_proj)
    )
    row3, side2 = shift_z(row2), swap_y(row2)
    down_other = swap_core(down_proj)
    home = send_home((1, 1), side1), send_home((2, 0), row2)
    row3, side2, strips[1, 1], strips[2, 0], down_other = barrier(
        (row3, side2, *home, down_other)
    )
    low, high = halves(row3, side0)
    low, high = barrier((low, high))
    low, high = swap_y(low), shift_z(high, -1)
    near = [chip for chip in CHIPS if chip in ((0, 1), (1, 0), (1, 1))]
    home = [hand_back(strips[chip], *chip) for chip in near]
    home += [send_home((2, 1), side2), send_home((3, 0), row3)]
    low, high, *home = barrier((low, high, *home))
    for chip, strip in zip(near + [(2, 1), (3, 0)], home):
        strips[chip] = strip
    send_home((3, 1), low, high)
    for chip in CHIPS:
        if chip not in near:
            strips[chip] = hand_back(strips[chip], *chip)
    attn, normed = normalise(up_chips, [strips[chip] for chip in CHIPS], norm_gain)

    gate_proj, up_proj, down_proj, normed = barrier((gate_proj, up_proj, down_proj, normed))
    row1, side0 = shift_z(normed), swap_y(normed)
    weights = [load(w) for w in (gate_proj, up_proj, down_proj)]
    weights += [gate_other, up_other, down_other]
    row1, side0, *weights = barrier((row1, side0, *weights))

    def run(r, *blocks):
        return expert(r, where, k_own, blocks, weights)

    row2, side1 = shift_z(row1), swap_y(row1)
    near0, far0 = run(0, normed, side0)
    row2, side1, near0, far0 = barrier((row2, side1, near0, far0))
    row3, side2 = shift_z(row2), swap_y(row2)
    near1, far1 = run(1, row1, side1)
    row3, side2, near1, far1 = barrier((row3, side2, near1, far1))
    side3, side1 = shift_z(side2), swap_y(far1)
    near2, far2 = run(2, row2, side2)
    side3, side1, near2, far2 = barrier((side3, side1, near2, far2))
    acc, side2 = shift_z(add(tok, 0, near1, side1)), swap_y(far2)
    near3, far3 = run(3, row3, side3)
    acc, side2, near3, far3 = barrier((acc, side2, near3, far3))
    acc, side3 = shift_z(add(tok, 0, acc, near2, side2)), swap_y(far3)
    acc, side3, far0 = barrier((acc, side3, far0))
    acc, side0 = shift_z(add(tok, 0, acc, near3, side3)), swap_y(far0)
    return add(tok, 0, attn, acc, near0, side0)


def solution(mesh):
    names = ("expert",)
    body = local
    shape = mesh.shape
    if shape["expert"] == NZ * NY * NC and shape["tensor"] == 1:
        groups = shape["groups"]
        mesh = Mesh(mesh.devices.reshape(groups, NZ, NY, NC, 1), ("groups", "z", "y", "core", "tensor"))
        names = ("z", "y", "core")
        body = boxed
    every = ("groups",) + names
    in_specs = (
        P(every, "tensor", None),
        P(every, None),
        P("tensor", names, None),
        P("tensor", names),
        P(),
        P(names, None, "tensor"),
        P(names, None, "tensor"),
        P(names, "tensor", None),
        P(every + ("tensor",), None),
        P(every + ("tensor",), None),
    )
    out_specs = P(every + ("tensor",), None)
    return jax.shard_map(body, mesh=mesh, in_specs=in_specs, out_specs=out_specs, check_vma=False)
```

```python
import jax
import jax.numpy as jnp
from jax import lax
from jax.experimental import pallas as pl
from jax.experimental.pallas import tpu as pltpu
from jax.sharding import Mesh, PartitionSpec as P

LAT = 256
VD = 128
TOP = 8
NZ, NY, NC = 4, 2, 2


score_scale = 0.0722


def local(
    queries,
    kv_latent,
    value_up,
    out_proj,
    norm_gain,
    gate_proj,
    up_proj,
    down_proj,
    routes,
    route_weights,
):
    tok, heads, width = queries.shape
    query_place = lax.axis_index("expert") * tok + jnp.arange(tok)
    piece = lax.all_gather(kv_latent, "expert", axis=0, tiled=True)
    running = jnp.full((tok, heads), -1e30, jnp.float32)
    count = piece.shape[0]
    scores = (
        jnp.einsum("shc,tc->sht", queries, piece, preferred_element_type=jnp.float32) * score_scale
    )
    key_place = jnp.arange(count)
    allowed = (query_place[:, None] >= key_place[None, :])[:, None, :]
    scores = jnp.where(allowed, scores, -1e30)
    newer = jnp.maximum(running, jnp.max(scores, axis=-1))
    expo = jnp.where(allowed, jnp.exp(scores - newer[..., None]), 0.0)
    total = jnp.sum(expo, axis=-1)
    update = jnp.einsum(
        "sht,tc->shc", expo.astype(jnp.bfloat16), piece[:, :LAT], preferred_element_type=jnp.float32
    )
    running, total, acc = (newer, total, update)
    latent_out = (acc / total[..., None]).astype(jnp.bfloat16)
    lifted = jnp.einsum(
        "shc,hcv->shv",
        latent_out,
        lax.all_gather(value_up, "expert", axis=1, tiled=True),
        preferred_element_type=jnp.float32,
    )
    flat_heads = lifted.astype(jnp.bfloat16).reshape(tok, heads * VD)
    partial_cols = jnp.dot(
        lax.all_gather(flat_heads, "expert", axis=0, tiled=True),
        out_proj,
        preferred_element_type=jnp.float32,
    )
    wide_rows = lax.all_to_all(
        partial_cols.astype(jnp.bfloat16), "expert", split_axis=0, concat_axis=1, tiled=True
    ).astype(partial_cols.dtype)
    attn = lax.psum_scatter(
        wide_rows.astype(jnp.bfloat16), "tensor", scatter_dimension=0, tiled=True
    )
    attn32 = attn.astype(jnp.float32)
    scale = lax.rsqrt(jnp.mean(attn32 * attn32, axis=-1, keepdims=True) + 1e-06)
    normed = (attn32 * scale * norm_gain).astype(jnp.bfloat16)
    rows = routes.shape[0]
    experts = lax.axis_size("expert") * gate_proj.shape[0]
    capacity = min(rows, max(2, 5 * rows * TOP // (4 * experts)))
    width_d = normed.shape[1]
    flat_routes = routes.reshape(-1)
    onehot = (flat_routes[:, None] == jnp.arange(experts)[None, :]).astype(jnp.int32)
    before = jnp.cumsum(onehot, axis=0) - onehot
    slot = jnp.sum(before * onehot, axis=1).reshape(rows, TOP)
    target = routes * capacity + slot
    slot_ids = jnp.arange(experts * capacity)
    placing = jnp.sum(
        (target[None, :, :] == slot_ids[:, None, None]).astype(jnp.int32), axis=2
    ).astype(jnp.bfloat16)
    outbound = jnp.dot(placing, normed, preferred_element_type=jnp.float32).astype(jnp.bfloat16)
    arrived = lax.all_to_all(
        outbound.reshape(experts, capacity, width_d),
        "expert",
        split_axis=0,
        concat_axis=0,
        tiled=True,
    )
    both_halves = lax.all_gather(arrived, "tensor", axis=0, tiled=True).reshape(-1, width_d)
    gate = jnp.dot(both_halves, gate_proj[0], preferred_element_type=jnp.float32)
    upper = jnp.dot(both_halves, up_proj[0], preferred_element_type=jnp.float32)
    hidden = (jax.nn.silu(gate) * upper).astype(jnp.bfloat16)
    down_terms = jnp.dot(hidden, down_proj[0], preferred_element_type=jnp.float32)
    expert_out = lax.psum_scatter(
        down_terms.astype(jnp.bfloat16), "tensor", scatter_dimension=0, tiled=True
    )
    back = lax.all_to_all(
        expert_out.reshape(experts, capacity, width_d),
        "expert",
        split_axis=0,
        concat_axis=0,
        tiled=True,
    )
    picked = back.reshape(-1, width_d)[target]
    mixed = jnp.sum(route_weights[:, :, None] * picked.astype(jnp.float32), axis=1)
    return (attn32 + mixed).astype(jnp.bfloat16)


CHIPS = [(r, b) for r in range(NZ) for b in range(NY)]
NT = (((1,), (1,)), ((), ()))
F32, B16 = jnp.float32, jnp.bfloat16
WHOLE = pl.BlockSpec(memory_space=pltpu.VMEM)
barrier = lax.optimization_barrier


def fold(at):
    return at ^ (at >> 1)


def step_z(z, by):
    return fold((fold(z) + by) % NZ)


def shift_z(value, by=1):
    return lax.ppermute(value, "z", [(z, step_z(z, by)) for z in range(NZ)])


def swap_y(value):
    return lax.ppermute(value, "y", [(0, 1), (1, 0)])


def swap_mate(value):
    return lax.ppermute(value, "z", [(z, z ^ 1) for z in range(NZ)])


def swap_group(value):
    return lax.ppermute(value, "groups", [(0, 1), (1, 0)])


def swap_core(value):
    return lax.ppermute(value, "core", [(0, 1), (1, 0)])


def hand_back(value, r, b):
    if r == 0 and b == 0:
        return value
    pairs = [
        (z * NY + y, step_z(z, -r) * NY + (y ^ b)) for z in range(NZ) for y in range(NY)
    ]
    return lax.ppermute(value, ("z", "y"), pairs)


def call(kernel, outs, scratch, limit, flops, name, *args):
    size = sum(a.size * a.dtype.itemsize for a in args)
    return pl.pallas_call(
        kernel,
        in_specs=[
            pl.BlockSpec(memory_space=pltpu.SMEM) if a.ndim == 1 else WHOLE for a in args
        ],
        out_specs=[WHOLE] * len(outs),
        out_shape=[
            jax.ShapeDtypeStruct(o, B16) if isinstance(o, tuple) else o for o in outs
        ],
        scratch_shapes=scratch,
        compiler_params=pltpu.CompilerParams(vmem_limit_bytes=limit << 20),
        cost_estimate=pl.CostEstimate(flops=flops, bytes_accessed=size, transcendentals=0),
        name=name,
    )(*args)


def prepare(where, kv_latent, routes, route_weights, value_up, experts):
    tok, width = kv_latent.shape
    heads, part, _ = value_up.shape
    half = heads // NC

    def kernel(where, kv, routed, weight, v, out, own, send):
        dense = jnp.zeros((experts, tok), F32)
        number = lax.broadcasted_iota(jnp.int32, (experts, tok), 0)
        for k in range(TOP):
            dense = dense + jnp.where(routed[k : k + 1] == number, weight[k : k + 1], 0.0)
        high = dense.astype(B16)
        low = (dense - high.astype(F32)).astype(B16)
        same = lax.broadcasted_iota(jnp.int32, (tok, tok), 0) == lax.broadcasted_iota(
            jnp.int32, (tok, tok), 1
        )
        eye = jnp.where(same, 1.0, 0.0).astype(B16)
        out[:, :width] = kv[...]
        for n, term in enumerate((high, low)):
            at = width + n * experts
            out[:, at : at + experts] = lax.dot_general(
                eye, term, NT, preferred_element_type=F32
            ).astype(B16)
        for at, ref in ((where[0], own), (1 - where[0], send)):
            ref[...] = v[pl.ds(pl.multiple_of(at * half, half), half)]

    return call(
        kernel,
        [(tok, width + 2 * experts)] + [(half, part, VD)] * 2,
        [],
        4,
        1 << 20,
        "prepare",
        where,
        kv_latent,
        routes.T,
        route_weights.T,
        value_up,
    )


def split_heads(where, queries):
    tok, heads, width = queries.shape
    half = heads // NC

    def kernel(where, q, own, send):
        for at, out in ((where[0], own), (1 - where[0], send)):
            first = pl.multiple_of(at * half, half)
            out[...] = jnp.swapaxes(q[:, pl.ds(first, half), :], 0, 1)

    shapes = [(half, tok, width)] * 2
    return call(kernel, shapes, [], 16, 1 << 16, "split_heads", where, queries)


def join_cores(where, own, other):
    heads, part, width = own.shape

    def kernel(where, a, b, out):
        out[:, pl.ds(pl.multiple_of(where[0] * part, part), part), :] = a[...]
        out[:, pl.ds(pl.multiple_of((1 - where[0]) * part, part), part), :] = b[...]

    return call(
        kernel, [(heads, 2 * part, width)], [], 4, 1 << 10, "join_cores", where, own, other
    )[0]


def stack_rows(blocks):
    rows, width = blocks[0].shape

    def kernel(*refs):
        for n, ref in enumerate(refs[:-1]):
            refs[-1][n * rows : (n + 1) * rows] = ref[...]

    return call(kernel, [(rows * len(blocks), width)], [], 2, 1 << 16, "stack_rows", *blocks)[0]


def attend(which, bases, q_own, q_other, k_own, k_other):
    heads, tok, width = q_own.shape
    heads = heads // 2
    half = k_own.shape[0]
    rows = 2 * tok
    hb, sub = 8, 2
    turn = score_scale * 1.4426950408889634

    def kernel(base, qo, qx, ko, kx, out, bias):
        step = lax.broadcasted_iota(jnp.int32, (tok, tok), 0) - lax.broadcasted_iota(
            jnp.int32, (tok, tok), 1
        )
        for d in range(2):
            for n in range(2 * half // tok):
                seen = jnp.where(step + (base[d] - base[2 + n]) >= 0, 0.0, -1e30)
                for j in range(sub):
                    at = j * rows + d * tok
                    bias[at : at + tok, n * tok : (n + 1) * tok] = seen
        own = base[2 + 2 * half // tok]
        first = (own if which == 0 else 1 - own) * heads

        def body(turns, _):
            at = turns * hb
            for g in range(0, hb, sub):
                q = jnp.concatenate(
                    [ref[first + at + j] for j in range(g, g + sub) for ref in (qo, qx)], axis=0
                )
                s0 = lax.dot_general(q, ko[:, :width], NT, preferred_element_type=F32)
                s1 = lax.dot_general(q, kx[:, :width], NT, preferred_element_type=F32)
                s0 = s0 + bias[:, :half]
                s1 = s1 + bias[:, half:]
                top = jnp.maximum(
                    jnp.max(s0, axis=-1, keepdims=True), jnp.max(s1, axis=-1, keepdims=True)
                )
                p0 = jnp.exp2((s0 - top) * turn)
                p1 = jnp.exp2((s1 - top) * turn)
                total = jnp.sum(p0, axis=-1, keepdims=True) + jnp.sum(p1, axis=-1, keepdims=True)
                acc = jnp.dot(p0.astype(B16), ko[:, :LAT], preferred_element_type=F32)
                acc = acc + jnp.dot(p1.astype(B16), kx[:, :LAT], preferred_element_type=F32)
                latent = (acc / total).astype(B16)
                for j in range(sub):
                    out[at + g + j] = latent[j * rows : (j + 1) * rows]
            return 0

        lax.fori_loop(0, heads // hb, body, 0)

    return call(
        kernel,
        [(heads, rows, LAT)],
        [pltpu.VMEM((sub * rows, 2 * half), F32)],
        16,
        2 * heads * rows * 2 * half * (width + LAT),
        "attend",
        bases,
        q_own,
        q_other,
        k_own,
        k_other,
    )[0]


def raise_values(which, where, chips, latent, pieces):
    heads, rows, _ = latent.shape
    part = pieces[0].shape[1]

    def kernel(where, chip, lat, *refs):
        parts, out, lift = refs[:-2], refs[-2], refs[-1]
        first = (where[1] if which == 0 else 1 - where[1]) * heads
        for at, ref in enumerate(parts):
            lift[:, pl.ds(pl.multiple_of(chip[at] * part, part), part), :] = ref[
                pl.ds(first, heads)
            ]
        for j in range(heads):
            out[:, j * VD : (j + 1) * VD] = jnp.dot(
                lat[j], lift[j], preferred_element_type=F32
            ).astype(B16)

    return call(
        kernel,
        [(rows, heads * VD)],
        [pltpu.VMEM((heads, LAT, VD), B16)],
        6,
        2 * heads * rows * LAT * VD,
        "raise_values",
        where,
        chips,
        latent,
        *pieces,
    )[0]


def split_proj(where, flat):
    cols, rows = flat.shape
    half = rows // NC

    def kernel(where, a, own, send):
        own[...] = a[:, pl.ds(pl.multiple_of(where[0] * half, half), half)]
        send[...] = a[:, pl.ds(pl.multiple_of((1 - where[0]) * half, half), half)]

    return call(kernel, [(cols, half)] * 2, [], 4, 1 << 16, "split_proj", where, flat)


def quarter_proj(where, own, other):
    cols, rows = own.shape
    half, part = rows // 2, rows // 8

    def kernel(where, a, b, keep, *sends):
        mine = pl.ds(pl.multiple_of(where[1] * half, half), half)
        start = (1 - where[1]) * half + where[2] * (2 * part)
        for ref, core in ((a, where[0]), (b, 1 - where[0])):
            at = pl.ds(pl.multiple_of(core * cols, 16), cols)
            keep[at, :] = ref[:, mine]
            for n, send in enumerate(sends):
                send[at, :] = ref[:, pl.ds(pl.multiple_of(start + n * part, part), part)]

    return call(
        kernel,
        [(2 * cols, half)] + [(2 * cols, part)] * 2,
        [],
        4,
        1 << 16,
        "quarter_proj",
        where,
        own,
        other,
    )


def join_proj(where, keep, came, across):
    cols, rows = keep.shape
    part = rows // 4

    def kernel(where, a, *refs):
        out = refs[-1]
        out[pl.ds(pl.multiple_of(where[3] * cols, 16), cols), :] = a[...]
        mate = pl.ds(pl.multiple_of((1 - where[3]) * cols, 16), cols)
        for n, ref in enumerate(refs[:-1]):
            group = where[2] if n < 2 else 1 - where[2]
            at = group * (2 * part) + (n % 2) * part
            out[mate, pl.ds(pl.multiple_of(at, part), part)] = ref[...]

    return call(
        kernel, [(2 * cols, rows)], [], 4, 1 << 16, "join_proj", where, keep, *came, *across
    )[0]


def halves(first, second):
    rows = first.shape[0] // 2

    def kernel(a, b, low, high):
        low[...] = a[:rows]
        high[...] = b[rows:]

    return call(kernel, [(rows, first.shape[1])] * 2, [], 2, 1 << 16, "halves", first, second)


def project(columns, *parts):
    rows = sum(part.shape[0] for part in parts)
    cols, depth = columns.shape
    tok = rows // 2

    def kernel(b, *refs):
        keep, send = refs[-2:]
        piece = jnp.concatenate([ref[...] for ref in refs[:-2]], axis=0)
        part = lax.dot_general(piece, b[...], NT, preferred_element_type=F32)
        keep[...] = part[:tok]
        send[...] = part[tok:].astype(B16)

    return call(
        kernel,
        [jax.ShapeDtypeStruct((tok, cols), F32), (tok, cols)],
        [],
        6,
        2 * rows * depth * cols,
        "project",
        columns,
        *parts,
    )


def add(rows, at, *terms):
    def kernel(*refs):
        total = 0.0
        for ref in refs[:-1]:
            block = ref[...] if ref.shape[0] == rows else ref[at : at + rows]
            total = total + block.astype(F32)
        refs[-1][...] = total.astype(B16)

    shape = (rows, terms[0].shape[1])
    return call(kernel, [shape], [], 4, rows * shape[1], "add", *terms)[0]


def normalise(chips, strips, norm_gain):
    tok, cols = strips[0].shape
    one = cols // 2
    wide = len(CHIPS) * one

    def kernel(chip, gain, *refs):
        parts, attn, normed, stage, full = refs[: len(CHIPS)], *refs[-4:]
        for n, ref in enumerate(parts):
            stage[chip[n]] = ref[...].astype(F32)
        for pair in range(NZ // 2):
            for y in range(NY):
                low = 2 * pair * NY + y
                both = stage[low] + stage[low + NY]
                full[:, low * one : (low + 1) * one] = both[:, :one]
                full[:, (low + NY) * one : (low + NY + 1) * one] = both[:, one:]
        rounded = full[...].astype(B16)
        attn[...] = rounded
        value = rounded.astype(F32)
        scale = lax.rsqrt(jnp.mean(value * value, axis=-1, keepdims=True) + 1e-06)
        normed[...] = (value * scale * gain[...]).astype(B16)

    return call(
        kernel,
        [(tok, wide)] * 2,
        [pltpu.VMEM((len(CHIPS), tok, cols), F32), pltpu.VMEM((tok, wide), F32)],
        10,
        1 << 20,
        "normalise",
        chips,
        norm_gain.reshape(1, -1),
        *strips,
    )


def load(weight):
    def kernel(source, out, sem):
        copy = pltpu.make_async_copy(source, out, sem)
        copy.start()
        copy.wait()

    return pl.pallas_call(
        kernel,
        in_specs=[pl.BlockSpec(memory_space=pltpu.HBM)],
        out_specs=WHOLE,
        out_shape=jax.ShapeDtypeStruct(weight.shape, weight.dtype),
        scratch_shapes=[pltpu.SemaphoreType.DMA],
        compiler_params=pltpu.CompilerParams(vmem_limit_bytes=2 << 20),
        cost_estimate=pl.CostEstimate(flops=0, bytes_accessed=weight.size * 2, transcendentals=0),
        name="load",
    )(weight)


def expert(r, where, k_own, blocks, weights):
    tok, width = blocks[0].shape
    units = weights[0].shape[2]
    fb, nb = 256, 512
    n = len(blocks)
    rows = n * tok
    dense = k_own.shape[1]
    experts = len(CHIPS) * NC

    def kernel(where, ko, *refs):
        mats, refs = refs[: 3 * NC], refs[3 * NC :]
        ins, outs, x, hidden, share = refs[:n], refs[n : 2 * n], *refs[2 * n :]
        lane = lax.broadcasted_iota(jnp.int32, (tok, 2 * experts), 1)
        for b in range(n):
            at = (b * NZ + r) * tok
            table = ko[at : at + tok, dense - 2 * experts :].astype(F32)
            for e in range(NC):
                number = where[4 + e]
                mine = (lane == number) | (lane == number + experts)
                share[b * tok : (b + 1) * tok, e : e + 1] = jnp.sum(
                    jnp.where(mine, table, 0.0), axis=-1, keepdims=True
                )
            x[b * tok : (b + 1) * tok] = ins[b][...]
        for e in range(NC):
            gate_w, up_w = mats[3 * e], mats[3 * e + 1]
            for f in range(0, units, fb):
                gate = jnp.dot(x[...], gate_w[0, :, f : f + fb], preferred_element_type=F32)
                upper = jnp.dot(x[...], up_w[0, :, f : f + fb], preferred_element_type=F32)
                hidden[e, :, f : f + fb] = (jax.nn.silu(gate) * upper).astype(B16)
        for c in range(0, width, nb):
            out = 0.0
            for e in range(NC):
                down = jnp.dot(
                    hidden[e], mats[3 * e + 2][0, :, c : c + nb], preferred_element_type=F32
                )
                out = out + down * share[:, e : e + 1]
            out = out.astype(B16)
            for b in range(n):
                outs[b][:, c : c + nb] = out[b * tok : (b + 1) * tok]

    return call(
        kernel,
        [(tok, width)] * n,
        [
            pltpu.VMEM((rows, width), B16),
            pltpu.VMEM((NC, rows, units), B16),
            pltpu.VMEM((rows, NC), F32),
        ],
        6,
        12 * rows * width * units,
        "expert",
        where,
        k_own,
        *weights,
        *blocks,
    )


def boxed(
    queries,
    kv_latent,
    value_up,
    out_proj,
    norm_gain,
    gate_proj,
    up_proj,
    down_proj,
    routes,
    route_weights,
):
    tok, heads, width = queries.shape
    group, z, y, core = (lax.axis_index(name) for name in ("groups", "z", "y", "core"))
    experts = NZ * NY * NC
    place = (z * NY + y) * NC + core
    kind = fold(z) % 2
    where = jnp.stack([core, kind, group, z % 2, place, place ^ 1]).astype(jnp.int32)
    up_chips = jnp.stack([step_z(z, r) * NY + (y ^ b) for r, b in CHIPS])
    down_chips = jnp.stack([step_z(z, -r) * NY + (y ^ b) for r, b in CHIPS])
    key_chips = jnp.stack([step_z(z, -r) * NY + (y ^ b) for b in range(NY) for r in range(NZ)])
    bases = [jnp.stack([place, place ^ 1]), key_chips * NC + core, key_chips * NC + (core ^ 1)]
    bases = jnp.concatenate([jnp.concatenate(bases) * tok, kind[None]]).astype(jnp.int32)
    where, up_chips, down_chips, bases, kv_latent = barrier(
        (where, up_chips, down_chips, bases, kv_latent)
    )

    pack, lift_own, lift_send = prepare(
        where, kv_latent, routes, route_weights, value_up, experts
    )
    queries, out_proj, pack = barrier((queries, out_proj, pack))
    keys = [pack] + [shift_z(pack, r) for r in range(1, NZ)]
    lift = join_cores(where, lift_own, swap_core(lift_send))
    queries, out_proj, lift = barrier((queries, out_proj, lift))
    up1, side0 = shift_z(lift), swap_y(lift)
    proj_own, proj_send = split_proj(where, out_proj.T)
    q_own, q_send = split_heads(where, queries)
    *keys, up1, side0, q_own, q_send, proj_own, proj_send = barrier(
        (*keys, up1, side0, q_own, q_send, proj_own, proj_send)
    )

    column = stack_rows(keys)
    beside = swap_y(column)
    up2 = shift_z(up1)
    q_other, proj_other = swap_core(q_send), swap_core(proj_send)
    beside, up2, up1, side0, q_other, proj_other = barrier(
        (beside, up2, up1, side0, q_other, proj_other)
    )

    k_own = stack_rows([column, beside])
    k_other = swap_core(k_own)
    up3, side1 = shift_z(up2), swap_y(up1)
    near = attend(0, bases, q_own, q_other, k_own, k_other)
    up3, side1, up2, near, q_own, proj_own, proj_other = barrier(
        (up3, side1, up2, near, q_own, proj_own, proj_other)
    )

    keep, send0, send1 = quarter_proj(where, proj_own, proj_other)
    send0, send1, q_own = barrier((send0, send1, q_own))
    side2, side3, came0 = swap_y(up2), swap_y(up3), swap_mate(send0)
    far = attend(1, bases, q_own, q_other, k_own, k_other)
    side2, side3, came0, far = barrier((side2, side3, came0, far))
    lifts = (lift, side0, up1, side1, up2, side2, up3, side3)
    near = raise_values(0, where, down_chips, near, lifts)
    far = raise_values(1, where, down_chips, far, lifts)

    high = halves(far, far)[1]
    near, far, high, send1, came0, gate_proj = barrier(
        (near, far, high, send1, came0, gate_proj)
    )
    row2, side0, high = shift_z(near, 2), swap_y(near), swap_y(high)
    came1, across0 = swap_mate(send1), swap_group(came0)
    gate_other = swap_core(gate_proj)
    row2, side0, high, came1, across0, gate_other = barrier(
        (row2, side0, high, came1, across0, gate_other)
    )
    row1, side2, across1 = shift_z(far), swap_y(row2), swap_group(came1)
    row1, side2, across1 = barrier((row1, side2, across1))
    row3, side1 = shift_z(far, -1), swap_y(row1)
    columns = join_proj(where, keep, (came0, came1), (across0, across1))
    parts = {(0, 0): project(columns, near)}
    up_other = swap_core(barrier((up_proj, parts[0, 0][0]))[0])
    for chip, piece in (((0, 1), side0), ((2, 0), row2), ((2, 1), side2), ((1, 0), row1)):
        parts[chip] = project(columns, piece)
    early = list(parts)
    row3, side1, *done = barrier((row3, side1, *(x for chip in early for x in parts[chip])))
    parts = {chip: done[2 * n : 2 * n + 2] for n, chip in enumerate(early)}
    low = halves(row3, row3)[0]
    low, high, row3, side1 = barrier((low, high, row3, side1))
    low, high = swap_y(low), shift_z(high, -1)
    parts[1, 1], parts[3, 0] = project(columns, side1), project(columns, row3)
    low, high, up_other, *done = barrier((low, high, up_other, *parts[1, 1], *parts[3, 0]))
    parts[1, 1], parts[3, 0] = done[:2], done[2:]
    parts[3, 1] = project(columns, low, high)
    mates = swap_core(stack_rows([parts[chip][1] for chip in CHIPS]))
    down_proj, mates = barrier((down_proj, mates))
    down_other = swap_core(down_proj)
    strips = {}
    for n, chip in enumerate(CHIPS):
        strips[chip] = hand_back(add(tok, n * tok, parts[chip][0], mates), *chip)
    attn, normed = normalise(up_chips, [strips[chip] for chip in CHIPS], norm_gain)

    gate_proj, up_proj, down_proj, normed = barrier((gate_proj, up_proj, down_proj, normed))
    row1, side0 = shift_z(normed), swap_y(normed)
    weights = [load(w) for w in (gate_proj, up_proj, down_proj)]
    weights += [gate_other, up_other, down_other]
    row1, side0, *weights = barrier((row1, side0, *weights))

    def run(r, *blocks):
        return expert(r, where, k_own, blocks, weights)

    row2, side1 = shift_z(row1), swap_y(row1)
    near0, far0 = run(0, normed, side0)
    row2, side1, near0, far0 = barrier((row2, side1, near0, far0))
    row3, side2 = shift_z(row2), swap_y(row2)
    near1, far1 = run(1, row1, side1)
    row3, side2, near1, far1 = barrier((row3, side2, near1, far1))
    side3, side1 = shift_z(side2), swap_y(far1)
    near2, far2 = run(2, row2, side2)
    side3, side1, near2, far2 = barrier((side3, side1, near2, far2))
    acc, side2 = shift_z(add(tok, 0, near1, side1)), swap_y(far2)
    near3, far3 = run(3, row3, side3)
    acc, side2, near3, far3 = barrier((acc, side2, near3, far3))
    acc, side3 = shift_z(add(tok, 0, acc, near2, side2)), swap_y(far3)
    acc, side3, far0 = barrier((acc, side3, far0))
    acc, side0 = shift_z(add(tok, 0, acc, near3, side3)), swap_y(far0)
    return add(tok, 0, attn, acc, near0, side0)


def solution(mesh):
    names = ("expert",)
    body = local
    shape = mesh.shape
    if shape["expert"] == NZ * NY * NC and shape["tensor"] == 1 and shape["groups"] == 2:
        mesh = Mesh(mesh.devices.reshape(2, NZ, NY, NC, 1), ("groups", "z", "y", "core", "tensor"))
        names = ("z", "y", "core")
        body = boxed
    every = ("groups",) + names
    in_specs = (
        P(every, "tensor", None),
        P(every, None),
        P("tensor", names, None),
        P("tensor", names),
        P(),
        P(names, None, "tensor"),
        P(names, None, "tensor"),
        P(names, "tensor", None),
        P(every + ("tensor",), None),
        P(every + ("tensor",), None),
    )
    out_specs = P(every + ("tensor",), None)
    return jax.shard_map(body, mesh=mesh, in_specs=in_specs, out_specs=out_specs, check_vma=False)
```

```python
import jax
import jax.numpy as jnp
from jax import lax
from jax.experimental import pallas as pl
from jax.experimental.pallas import tpu as pltpu
from jax.sharding import Mesh, PartitionSpec as P

LAT = 256
VD = 128
TOP = 8
NZ, NY, NC = 4, 2, 2


score_scale = 0.0722


def local(
    queries,
    kv_latent,
    value_up,
    out_proj,
    norm_gain,
    gate_proj,
    up_proj,
    down_proj,
    routes,
    route_weights,
):
    tok, heads, width = queries.shape
    query_place = lax.axis_index("expert") * tok + jnp.arange(tok)
    piece = lax.all_gather(kv_latent, "expert", axis=0, tiled=True)
    running = jnp.full((tok, heads), -1e30, jnp.float32)
    count = piece.shape[0]
    scores = (
        jnp.einsum("shc,tc->sht", queries, piece, preferred_element_type=jnp.float32) * score_scale
    )
    key_place = jnp.arange(count)
    allowed = (query_place[:, None] >= key_place[None, :])[:, None, :]
    scores = jnp.where(allowed, scores, -1e30)
    newer = jnp.maximum(running, jnp.max(scores, axis=-1))
    expo = jnp.where(allowed, jnp.exp(scores - newer[..., None]), 0.0)
    total = jnp.sum(expo, axis=-1)
    update = jnp.einsum(
        "sht,tc->shc", expo.astype(jnp.bfloat16), piece[:, :LAT], preferred_element_type=jnp.float32
    )
    running, total, acc = (newer, total, update)
    latent_out = (acc / total[..., None]).astype(jnp.bfloat16)
    lifted = jnp.einsum(
        "shc,hcv->shv",
        latent_out,
        lax.all_gather(value_up, "expert", axis=1, tiled=True),
        preferred_element_type=jnp.float32,
    )
    flat_heads = lifted.astype(jnp.bfloat16).reshape(tok, heads * VD)
    partial_cols = jnp.dot(
        lax.all_gather(flat_heads, "expert", axis=0, tiled=True),
        out_proj,
        preferred_element_type=jnp.float32,
    )
    wide_rows = lax.all_to_all(
        partial_cols.astype(jnp.bfloat16), "expert", split_axis=0, concat_axis=1, tiled=True
    ).astype(partial_cols.dtype)
    attn = lax.psum_scatter(
        wide_rows.astype(jnp.bfloat16), "tensor", scatter_dimension=0, tiled=True
    )
    attn32 = attn.astype(jnp.float32)
    scale = lax.rsqrt(jnp.mean(attn32 * attn32, axis=-1, keepdims=True) + 1e-06)
    normed = (attn32 * scale * norm_gain).astype(jnp.bfloat16)
    rows = routes.shape[0]
    experts = lax.axis_size("expert") * gate_proj.shape[0]
    capacity = min(rows, max(2, 5 * rows * TOP // (4 * experts)))
    width_d = normed.shape[1]
    flat_routes = routes.reshape(-1)
    onehot = (flat_routes[:, None] == jnp.arange(experts)[None, :]).astype(jnp.int32)
    before = jnp.cumsum(onehot, axis=0) - onehot
    slot = jnp.sum(before * onehot, axis=1).reshape(rows, TOP)
    target = routes * capacity + slot
    slot_ids = jnp.arange(experts * capacity)
    placing = jnp.sum(
        (target[None, :, :] == slot_ids[:, None, None]).astype(jnp.int32), axis=2
    ).astype(jnp.bfloat16)
    outbound = jnp.dot(placing, normed, preferred_element_type=jnp.float32).astype(jnp.bfloat16)
    arrived = lax.all_to_all(
        outbound.reshape(experts, capacity, width_d),
        "expert",
        split_axis=0,
        concat_axis=0,
        tiled=True,
    )
    both_halves = lax.all_gather(arrived, "tensor", axis=0, tiled=True).reshape(-1, width_d)
    gate = jnp.dot(both_halves, gate_proj[0], preferred_element_type=jnp.float32)
    upper = jnp.dot(both_halves, up_proj[0], preferred_element_type=jnp.float32)
    hidden = (jax.nn.silu(gate) * upper).astype(jnp.bfloat16)
    down_terms = jnp.dot(hidden, down_proj[0], preferred_element_type=jnp.float32)
    expert_out = lax.psum_scatter(
        down_terms.astype(jnp.bfloat16), "tensor", scatter_dimension=0, tiled=True
    )
    back = lax.all_to_all(
        expert_out.reshape(experts, capacity, width_d),
        "expert",
        split_axis=0,
        concat_axis=0,
        tiled=True,
    )
    picked = back.reshape(-1, width_d)[target]
    mixed = jnp.sum(route_weights[:, :, None] * picked.astype(jnp.float32), axis=1)
    return (attn32 + mixed).astype(jnp.bfloat16)


CHIPS = [(r, b) for r in range(NZ) for b in range(NY)]
NT = (((1,), (1,)), ((), ()))
F32, B16 = jnp.float32, jnp.bfloat16
WHOLE = pl.BlockSpec(memory_space=pltpu.VMEM)
barrier = lax.optimization_barrier


def fold(at):
    return at ^ (at >> 1)


def step_z(z, by):
    return fold((fold(z) + by) % NZ)


def shift_z(value, by=1):
    return lax.ppermute(value, "z", [(z, step_z(z, by)) for z in range(NZ)])


def swap_y(value):
    return lax.ppermute(value, "y", [(0, 1), (1, 0)])


def swap_mate(value):
    return lax.ppermute(value, "z", [(z, z ^ 1) for z in range(NZ)])


def swap_group(value):
    return lax.ppermute(value, "groups", [(0, 1), (1, 0)])


def swap_core(value):
    return lax.ppermute(value, "core", [(0, 1), (1, 0)])


def hand_back(value, r, b):
    if r == 0 and b == 0:
        return value
    pairs = [
        (z * NY + y, step_z(z, -r) * NY + (y ^ b)) for z in range(NZ) for y in range(NY)
    ]
    return lax.ppermute(value, ("z", "y"), pairs)


def call(kernel, outs, scratch, limit, flops, name, *args):
    size = sum(a.size * a.dtype.itemsize for a in args)
    return pl.pallas_call(
        kernel,
        in_specs=[
            pl.BlockSpec(memory_space=pltpu.SMEM) if a.ndim == 1 else WHOLE for a in args
        ],
        out_specs=[WHOLE] * len(outs),
        out_shape=[
            jax.ShapeDtypeStruct(o, B16) if isinstance(o, tuple) else o for o in outs
        ],
        scratch_shapes=scratch,
        compiler_params=pltpu.CompilerParams(vmem_limit_bytes=limit << 20),
        cost_estimate=pl.CostEstimate(flops=flops, bytes_accessed=size, transcendentals=0),
        name=name,
    )(*args)


def prepare(where, kv_latent, routes, route_weights, value_up, experts):
    tok, width = kv_latent.shape
    heads, part, _ = value_up.shape
    half = heads // NC

    def kernel(where, kv, routed, weight, v, out, own, send):
        dense = jnp.zeros((experts, tok), F32)
        number = lax.broadcasted_iota(jnp.int32, (experts, tok), 0)
        for k in range(TOP):
            dense = dense + jnp.where(routed[k : k + 1] == number, weight[k : k + 1], 0.0)
        high = dense.astype(B16)
        low = (dense - high.astype(F32)).astype(B16)
        same = lax.broadcasted_iota(jnp.int32, (tok, tok), 0) == lax.broadcasted_iota(
            jnp.int32, (tok, tok), 1
        )
        eye = jnp.where(same, 1.0, 0.0).astype(B16)
        out[:, :width] = kv[...]
        for n, term in enumerate((high, low)):
            at = width + n * experts
            out[:, at : at + experts] = lax.dot_general(
                eye, term, NT, preferred_element_type=F32
            ).astype(B16)
        for at, ref in ((where[0], own), (1 - where[0], send)):
            ref[...] = v[pl.ds(pl.multiple_of(at * half, half), half)]

    return call(
        kernel,
        [(tok, width + 2 * experts)] + [(half, part, VD)] * 2,
        [],
        4,
        1 << 20,
        "prepare",
        where,
        kv_latent,
        routes.T,
        route_weights.T,
        value_up,
    )


def split_heads(where, queries):
    tok, heads, width = queries.shape
    half = heads // NC

    def kernel(where, q, own, send):
        for at, out in ((where[0], own), (1 - where[0], send)):
            first = pl.multiple_of(at * half, half)
            out[...] = jnp.swapaxes(q[:, pl.ds(first, half), :], 0, 1)

    shapes = [(half, tok, width)] * 2
    return call(kernel, shapes, [], 16, 1 << 16, "split_heads", where, queries)


def join_cores(where, own, other):
    heads, part, width = own.shape

    def kernel(where, a, b, out):
        out[:, pl.ds(pl.multiple_of(where[0] * part, part), part), :] = a[...]
        out[:, pl.ds(pl.multiple_of((1 - where[0]) * part, part), part), :] = b[...]

    return call(
        kernel, [(heads, 2 * part, width)], [], 4, 1 << 10, "join_cores", where, own, other
    )[0]


def stack_rows(blocks):
    rows, width = blocks[0].shape

    def kernel(*refs):
        for n, ref in enumerate(refs[:-1]):
            refs[-1][n * rows : (n + 1) * rows] = ref[...]

    return call(kernel, [(rows * len(blocks), width)], [], 2, 1 << 16, "stack_rows", *blocks)[0]


def attend(which, bases, q_own, q_other, k_own, k_other):
    heads, tok, width = q_own.shape
    heads = heads // 2
    half = k_own.shape[0]
    rows = 2 * tok
    hb, sub = 8, 2
    turn = score_scale * 1.4426950408889634

    def kernel(base, qo, qx, ko, kx, out, bias):
        step = lax.broadcasted_iota(jnp.int32, (tok, tok), 0) - lax.broadcasted_iota(
            jnp.int32, (tok, tok), 1
        )
        for d in range(2):
            for n in range(2 * half // tok):
                seen = jnp.where(step + (base[d] - base[2 + n]) >= 0, 0.0, -1e30)
                for j in range(sub):
                    at = j * rows + d * tok
                    bias[at : at + tok, n * tok : (n + 1) * tok] = seen
        own = base[2 + 2 * half // tok]
        first = (own if which == 0 else 1 - own) * heads

        def body(turns, _):
            at = turns * hb
            for g in range(0, hb, sub):
                q = jnp.concatenate(
                    [ref[first + at + j] for j in range(g, g + sub) for ref in (qo, qx)], axis=0
                )
                s0 = lax.dot_general(q, ko[:, :width], NT, preferred_element_type=F32)
                s1 = lax.dot_general(q, kx[:, :width], NT, preferred_element_type=F32)
                s0 = s0 + bias[:, :half]
                s1 = s1 + bias[:, half:]
                top = jnp.maximum(
                    jnp.max(s0, axis=-1, keepdims=True), jnp.max(s1, axis=-1, keepdims=True)
                )
                p0 = jnp.exp2((s0 - top) * turn)
                p1 = jnp.exp2((s1 - top) * turn)
                total = jnp.sum(p0, axis=-1, keepdims=True) + jnp.sum(p1, axis=-1, keepdims=True)
                acc = jnp.dot(p0.astype(B16), ko[:, :LAT], preferred_element_type=F32)
                acc = acc + jnp.dot(p1.astype(B16), kx[:, :LAT], preferred_element_type=F32)
                latent = (acc / total).astype(B16)
                for j in range(sub):
                    out[at + g + j] = latent[j * rows : (j + 1) * rows]
            return 0

        lax.fori_loop(0, heads // hb, body, 0)

    return call(
        kernel,
        [(heads, rows, LAT)],
        [pltpu.VMEM((sub * rows, 2 * half), F32)],
        16,
        2 * heads * rows * 2 * half * (width + LAT),
        "attend",
        bases,
        q_own,
        q_other,
        k_own,
        k_other,
    )[0]


def raise_values(which, where, chips, latent, pieces):
    heads, rows, _ = latent.shape
    part = pieces[0].shape[1]

    def kernel(where, chip, lat, *refs):
        parts, out, lift = refs[:-2], refs[-2], refs[-1]
        first = (where[1] if which == 0 else 1 - where[1]) * heads
        for at, ref in enumerate(parts):
            lift[:, pl.ds(pl.multiple_of(chip[at] * part, part), part), :] = ref[
                pl.ds(first, heads)
            ]
        for j in range(heads):
            out[:, j * VD : (j + 1) * VD] = jnp.dot(
                lat[j], lift[j], preferred_element_type=F32
            ).astype(B16)

    return call(
        kernel,
        [(rows, heads * VD)],
        [pltpu.VMEM((heads, LAT, VD), B16)],
        6,
        2 * heads * rows * LAT * VD,
        "raise_values",
        where,
        chips,
        latent,
        *pieces,
    )[0]


def split_proj(where, flat):
    cols, rows = flat.shape
    half = rows // NC

    def kernel(where, a, own, send):
        own[...] = a[:, pl.ds(pl.multiple_of(where[0] * half, half), half)]
        send[...] = a[:, pl.ds(pl.multiple_of((1 - where[0]) * half, half), half)]

    return call(kernel, [(cols, half)] * 2, [], 4, 1 << 16, "split_proj", where, flat)


def quarter_proj(where, own, other):
    cols, rows = own.shape
    half, part = rows // 2, rows // 8

    def kernel(where, a, b, keep, *sends):
        mine = pl.ds(pl.multiple_of(where[1] * half, half), half)
        start = (1 - where[1]) * half + where[2] * (2 * part)
        for ref, core in ((a, where[0]), (b, 1 - where[0])):
            at = pl.ds(pl.multiple_of(core * cols, 16), cols)
            keep[at, :] = ref[:, mine]
            for n, send in enumerate(sends):
                send[at, :] = ref[:, pl.ds(pl.multiple_of(start + n * part, part), part)]

    return call(
        kernel,
        [(2 * cols, half)] + [(2 * cols, part)] * 2,
        [],
        4,
        1 << 16,
        "quarter_proj",
        where,
        own,
        other,
    )


def join_proj(where, keep, came, across):
    cols, rows = keep.shape
    part = rows // 4

    def kernel(where, a, *refs):
        out = refs[-1]
        out[pl.ds(pl.multiple_of(where[3] * cols, 16), cols), :] = a[...]
        mate = pl.ds(pl.multiple_of((1 - where[3]) * cols, 16), cols)
        for n, ref in enumerate(refs[:-1]):
            group = where[2] if n < 2 else 1 - where[2]
            at = group * (2 * part) + (n % 2) * part
            out[mate, pl.ds(pl.multiple_of(at, part), part)] = ref[...]

    return call(
        kernel, [(2 * cols, rows)], [], 4, 1 << 16, "join_proj", where, keep, *came, *across
    )[0]


def halves(first, second):
    rows = first.shape[0] // 2

    def kernel(a, b, low, high):
        low[...] = a[:rows]
        high[...] = b[rows:]

    return call(kernel, [(rows, first.shape[1])] * 2, [], 2, 1 << 16, "halves", first, second)


def project(columns, *parts):
    rows = sum(part.shape[0] for part in parts)
    cols, depth = columns.shape
    tok = rows // 2

    def kernel(b, *refs):
        keep, send = refs[-2:]
        piece = jnp.concatenate([ref[...] for ref in refs[:-2]], axis=0)
        part = lax.dot_general(piece, b[...], NT, preferred_element_type=F32)
        keep[...] = part[:tok]
        send[...] = part[tok:].astype(B16)

    return call(
        kernel,
        [jax.ShapeDtypeStruct((tok, cols), F32), (tok, cols)],
        [],
        6,
        2 * rows * depth * cols,
        "project",
        columns,
        *parts,
    )


def add(rows, at, *terms):
    def kernel(*refs):
        total = 0.0
        for ref in refs[:-1]:
            block = ref[...] if ref.shape[0] == rows else ref[at : at + rows]
            total = total + block.astype(F32)
        refs[-1][...] = total.astype(B16)

    shape = (rows, terms[0].shape[1])
    return call(kernel, [shape], [], 4, rows * shape[1], "add", *terms)[0]


def sum_strips(kept, mates):
    tok, cols = kept[0].shape
    count = len(kept)

    def kernel(*refs):
        others, outs = refs[count], refs[count + 1 :]
        for n in range(count):
            part = refs[n][...] + others[n * tok : (n + 1) * tok].astype(F32)
            outs[n][...] = part.astype(B16)

    shapes = [(tok, cols)] * count
    return call(kernel, shapes, [], 4, count * tok * cols, "sum_strips", *kept, mates)


def normalise(chips, strips, norm_gain):
    tok, cols = strips[0].shape
    one = cols // 2
    wide = len(CHIPS) * one

    def kernel(chip, gain, *refs):
        parts, attn, normed, stage, full = refs[: len(CHIPS)], *refs[-4:]
        for n, ref in enumerate(parts):
            stage[chip[n]] = ref[...].astype(F32)
        for pair in range(NZ // 2):
            for y in range(NY):
                low = 2 * pair * NY + y
                both = stage[low] + stage[low + NY]
                full[:, low * one : (low + 1) * one] = both[:, :one]
                full[:, (low + NY) * one : (low + NY + 1) * one] = both[:, one:]
        rounded = full[...].astype(B16)
        attn[...] = rounded
        value = rounded.astype(F32)
        scale = lax.rsqrt(jnp.mean(value * value, axis=-1, keepdims=True) + 1e-06)
        normed[...] = (value * scale * gain[...]).astype(B16)

    return call(
        kernel,
        [(tok, wide)] * 2,
        [pltpu.VMEM((len(CHIPS), tok, cols), F32), pltpu.VMEM((tok, wide), F32)],
        10,
        1 << 20,
        "normalise",
        chips,
        norm_gain.reshape(1, -1),
        *strips,
    )


def load(weight):
    def kernel(source, out, sem):
        copy = pltpu.make_async_copy(source, out, sem)
        copy.start()
        copy.wait()

    return pl.pallas_call(
        kernel,
        in_specs=[pl.BlockSpec(memory_space=pltpu.HBM)],
        out_specs=WHOLE,
        out_shape=jax.ShapeDtypeStruct(weight.shape, weight.dtype),
        scratch_shapes=[pltpu.SemaphoreType.DMA],
        compiler_params=pltpu.CompilerParams(vmem_limit_bytes=2 << 20),
        cost_estimate=pl.CostEstimate(flops=0, bytes_accessed=weight.size * 2, transcendentals=0),
        name="load",
    )(weight)


def expert(r, where, k_own, blocks, weights):
    tok, width = blocks[0].shape
    units = weights[0].shape[2]
    fb, nb = 256, 512
    n = len(blocks)
    rows = n * tok
    dense = k_own.shape[1]
    experts = len(CHIPS) * NC

    def kernel(where, ko, *refs):
        mats, refs = refs[: 3 * NC], refs[3 * NC :]
        ins, outs, x, hidden, share = refs[:n], refs[n : 2 * n], *refs[2 * n :]
        lane = lax.broadcasted_iota(jnp.int32, (tok, 2 * experts), 1)
        for b in range(n):
            at = (b * NZ + r) * tok
            table = ko[at : at + tok, dense - 2 * experts :].astype(F32)
            for e in range(NC):
                number = where[4 + e]
                mine = (lane == number) | (lane == number + experts)
                share[b * tok : (b + 1) * tok, e : e + 1] = jnp.sum(
                    jnp.where(mine, table, 0.0), axis=-1, keepdims=True
                )
            x[b * tok : (b + 1) * tok] = ins[b][...]
        for e in range(NC):
            gate_w, up_w = mats[3 * e], mats[3 * e + 1]
            for f in range(0, units, fb):
                gate = jnp.dot(x[...], gate_w[0, :, f : f + fb], preferred_element_type=F32)
                upper = jnp.dot(x[...], up_w[0, :, f : f + fb], preferred_element_type=F32)
                hidden[e, :, f : f + fb] = (jax.nn.silu(gate) * upper).astype(B16)
        for c in range(0, width, nb):
            out = 0.0
            for e in range(NC):
                down = jnp.dot(
                    hidden[e], mats[3 * e + 2][0, :, c : c + nb], preferred_element_type=F32
                )
                out = out + down * share[:, e : e + 1]
            out = out.astype(B16)
            for b in range(n):
                outs[b][:, c : c + nb] = out[b * tok : (b + 1) * tok]

    return call(
        kernel,
        [(tok, width)] * n,
        [
            pltpu.VMEM((rows, width), B16),
            pltpu.VMEM((NC, rows, units), B16),
            pltpu.VMEM((rows, NC), F32),
        ],
        6,
        12 * rows * width * units,
        "expert",
        where,
        k_own,
        *weights,
        *blocks,
    )


def boxed(
    queries,
    kv_latent,
    value_up,
    out_proj,
    norm_gain,
    gate_proj,
    up_proj,
    down_proj,
    routes,
    route_weights,
):
    tok, heads, width = queries.shape
    group, z, y, core = (lax.axis_index(name) for name in ("groups", "z", "y", "core"))
    experts = NZ * NY * NC
    place = (z * NY + y) * NC + core
    kind = fold(z) % 2
    where = jnp.stack([core, kind, group, z % 2, place, place ^ 1]).astype(jnp.int32)
    up_chips = jnp.stack([step_z(z, r) * NY + (y ^ b) for r, b in CHIPS])
    down_chips = jnp.stack([step_z(z, -r) * NY + (y ^ b) for r, b in CHIPS])
    key_chips = jnp.stack([step_z(z, -r) * NY + (y ^ b) for b in range(NY) for r in range(NZ)])
    bases = [jnp.stack([place, place ^ 1]), key_chips * NC + core, key_chips * NC + (core ^ 1)]
    bases = jnp.concatenate([jnp.concatenate(bases) * tok, kind[None]]).astype(jnp.int32)
    where, up_chips, down_chips, bases, kv_latent = barrier(
        (where, up_chips, down_chips, bases, kv_latent)
    )

    pack, lift_own, lift_send = prepare(
        where, kv_latent, routes, route_weights, value_up, experts
    )
    queries, out_proj, pack = barrier((queries, out_proj, pack))
    keys = [pack] + [shift_z(pack, r) for r in range(1, NZ)]
    lift = join_cores(where, lift_own, swap_core(lift_send))
    queries, out_proj, lift = barrier((queries, out_proj, lift))
    up1, side0 = shift_z(lift), swap_y(lift)
    proj_own, proj_send = split_proj(where, out_proj.T)
    q_own, q_send = split_heads(where, queries)
    *keys, up1, side0, q_own, q_send, proj_own, proj_send = barrier(
        (*keys, up1, side0, q_own, q_send, proj_own, proj_send)
    )

    column = stack_rows(keys)
    beside = swap_y(column)
    up2 = shift_z(up1)
    q_other, proj_other = swap_core(q_send), swap_core(proj_send)
    beside, up2, up1, side0, q_other, proj_other = barrier(
        (beside, up2, up1, side0, q_other, proj_other)
    )

    k_own = stack_rows([column, beside])
    k_other = swap_core(k_own)
    up3, side1 = shift_z(up2), swap_y(up1)
    near = attend(0, bases, q_own, q_other, k_own, k_other)
    up3, side1, up2, near, q_own, proj_own, proj_other = barrier(
        (up3, side1, up2, near, q_own, proj_own, proj_other)
    )

    keep, send0, send1 = quarter_proj(where, proj_own, proj_other)
    send0, send1, q_own = barrier((send0, send1, q_own))
    side2, side3, came0 = swap_y(up2), swap_y(up3), swap_mate(send0)
    far = attend(1, bases, q_own, q_other, k_own, k_other)
    side2, side3, came0, far = barrier((side2, side3, came0, far))
    lifts = (lift, side0, up1, side1, up2, side2, up3, side3)
    near = raise_values(0, where, down_chips, near, lifts)

    near, far, send1, came0, gate_proj = barrier((near, far, send1, came0, gate_proj))
    row2, side0 = shift_z(near, 2), swap_y(near)
    far = raise_values(1, where, down_chips, far, lifts)
    high = swap_y(halves(far, far)[1])
    came1, across0 = swap_mate(send1), swap_group(came0)
    gate_other = swap_core(gate_proj)
    row2, side0, high, came1, across0, gate_other = barrier(
        (row2, side0, high, came1, across0, gate_other)
    )
    row1, side2, across1 = shift_z(far), swap_y(row2), swap_group(came1)
    row1, side2, across1, up_proj = barrier((row1, side2, across1, up_proj))
    up_other = swap_core(up_proj)
    row3, side1 = shift_z(far, -1), swap_y(row1)
    columns = join_proj(where, keep, (came0, came1), (across0, across1))
    parts = {(0, 0): project(columns, near)}
    for chip, piece in (((0, 1), side0), ((2, 0), row2), ((2, 1), side2), ((1, 0), row1)):
        parts[chip] = project(columns, piece)
    early = list(parts)
    row3, side1, *done = barrier((row3, side1, *(x for chip in early for x in parts[chip])))
    parts = {chip: done[2 * n : 2 * n + 2] for n, chip in enumerate(early)}
    low = halves(row3, row3)[0]
    low, high, row3, side1 = barrier((low, high, row3, side1))
    low, high = swap_y(low), shift_z(high, -1)
    parts[1, 1], parts[3, 0] = project(columns, side1), project(columns, row3)
    low, high, up_other, *done = barrier((low, high, up_other, *parts[1, 1], *parts[3, 0]))
    parts[1, 1], parts[3, 0] = done[:2], done[2:]
    parts[3, 1] = project(columns, low, high)
    mates = swap_core(stack_rows([parts[chip][1] for chip in CHIPS]))
    down_proj, mates = barrier((down_proj, mates))
    down_other = swap_core(down_proj)
    sums = sum_strips([parts[chip][0] for chip in CHIPS], mates)
    strips = {chip: hand_back(total, *chip) for chip, total in zip(CHIPS, sums)}
    attn, normed = normalise(up_chips, [strips[chip] for chip in CHIPS], norm_gain)

    gate_proj, up_proj, down_proj, normed = barrier((gate_proj, up_proj, down_proj, normed))
    row1, side0 = shift_z(normed), swap_y(normed)
    weights = [load(w) for w in (gate_proj, up_proj, down_proj)]
    weights += [gate_other, up_other, down_other]
    row1, side0, *weights = barrier((row1, side0, *weights))

    def run(r, *blocks):
        return expert(r, where, k_own, blocks, weights)

    row2, side1 = shift_z(row1), swap_y(row1)
    near0, far0 = run(0, normed, side0)
    row2, side1, near0, far0 = barrier((row2, side1, near0, far0))
    row3, side2 = shift_z(row2), swap_y(row2)
    near1, far1 = run(1, row1, side1)
    row3, side2, near1, far1 = barrier((row3, side2, near1, far1))
    side3, side1 = shift_z(side2), swap_y(far1)
    near2, far2 = run(2, row2, side2)
    side3, side1, near2, far2 = barrier((side3, side1, near2, far2))
    acc, side2 = shift_z(add(tok, 0, near1, side1)), swap_y(far2)
    near3, far3 = run(3, row3, side3)
    acc, side2, near3, far3 = barrier((acc, side2, near3, far3))
    acc, side3 = shift_z(add(tok, 0, acc, near2, side2)), swap_y(far3)
    acc, side3, far0 = barrier((acc, side3, far0))
    acc, side0 = shift_z(add(tok, 0, acc, near3, side3)), swap_y(far0)
    return add(tok, 0, attn, acc, near0, side0)


def solution(mesh):
    names = ("expert",)
    body = local
    shape = mesh.shape
    if shape["expert"] == NZ * NY * NC and shape["tensor"] == 1 and shape["groups"] == 2:
        mesh = Mesh(mesh.devices.reshape(2, NZ, NY, NC, 1), ("groups", "z", "y", "core", "tensor"))
        names = ("z", "y", "core")
        body = boxed
    every = ("groups",) + names
    in_specs = (
        P(every, "tensor", None),
        P(every, None),
        P("tensor", names, None),
        P("tensor", names),
        P(),
        P(names, None, "tensor"),
        P(names, None, "tensor"),
        P(names, "tensor", None),
        P(every + ("tensor",), None),
        P(every + ("tensor",), None),
    )
    out_specs = P(every + ("tensor",), None)
    return jax.shard_map(body, mesh=mesh, in_specs=in_specs, out_specs=out_specs, check_vma=False)
```

```python
import jax
import jax.numpy as jnp
from jax import lax
from jax.experimental import pallas as pl
from jax.experimental.pallas import tpu as pltpu
from jax.sharding import Mesh, PartitionSpec as P

LAT = 256
VD = 128
TOP = 8
NZ, NY, NC = 4, 2, 2


score_scale = 0.0722


def local(
    queries,
    kv_latent,
    value_up,
    out_proj,
    norm_gain,
    gate_proj,
    up_proj,
    down_proj,
    routes,
    route_weights,
):
    tok, heads, width = queries.shape
    query_place = lax.axis_index("expert") * tok + jnp.arange(tok)
    piece = lax.all_gather(kv_latent, "expert", axis=0, tiled=True)
    running = jnp.full((tok, heads), -1e30, jnp.float32)
    count = piece.shape[0]
    scores = (
        jnp.einsum("shc,tc->sht", queries, piece, preferred_element_type=jnp.float32) * score_scale
    )
    key_place = jnp.arange(count)
    allowed = (query_place[:, None] >= key_place[None, :])[:, None, :]
    scores = jnp.where(allowed, scores, -1e30)
    newer = jnp.maximum(running, jnp.max(scores, axis=-1))
    expo = jnp.where(allowed, jnp.exp(scores - newer[..., None]), 0.0)
    total = jnp.sum(expo, axis=-1)
    update = jnp.einsum(
        "sht,tc->shc", expo.astype(jnp.bfloat16), piece[:, :LAT], preferred_element_type=jnp.float32
    )
    running, total, acc = (newer, total, update)
    latent_out = (acc / total[..., None]).astype(jnp.bfloat16)
    lifted = jnp.einsum(
        "shc,hcv->shv",
        latent_out,
        lax.all_gather(value_up, "expert", axis=1, tiled=True),
        preferred_element_type=jnp.float32,
    )
    flat_heads = lifted.astype(jnp.bfloat16).reshape(tok, heads * VD)
    partial_cols = jnp.dot(
        lax.all_gather(flat_heads, "expert", axis=0, tiled=True),
        out_proj,
        preferred_element_type=jnp.float32,
    )
    wide_rows = lax.all_to_all(
        partial_cols.astype(jnp.bfloat16), "expert", split_axis=0, concat_axis=1, tiled=True
    ).astype(partial_cols.dtype)
    attn = lax.psum_scatter(
        wide_rows.astype(jnp.bfloat16), "tensor", scatter_dimension=0, tiled=True
    )
    attn32 = attn.astype(jnp.float32)
    scale = lax.rsqrt(jnp.mean(attn32 * attn32, axis=-1, keepdims=True) + 1e-06)
    normed = (attn32 * scale * norm_gain).astype(jnp.bfloat16)
    rows = routes.shape[0]
    experts = lax.axis_size("expert") * gate_proj.shape[0]
    capacity = min(rows, max(2, 5 * rows * TOP // (4 * experts)))
    width_d = normed.shape[1]
    flat_routes = routes.reshape(-1)
    onehot = (flat_routes[:, None] == jnp.arange(experts)[None, :]).astype(jnp.int32)
    before = jnp.cumsum(onehot, axis=0) - onehot
    slot = jnp.sum(before * onehot, axis=1).reshape(rows, TOP)
    target = routes * capacity + slot
    slot_ids = jnp.arange(experts * capacity)
    placing = jnp.sum(
        (target[None, :, :] == slot_ids[:, None, None]).astype(jnp.int32), axis=2
    ).astype(jnp.bfloat16)
    outbound = jnp.dot(placing, normed, preferred_element_type=jnp.float32).astype(jnp.bfloat16)
    arrived = lax.all_to_all(
        outbound.reshape(experts, capacity, width_d),
        "expert",
        split_axis=0,
        concat_axis=0,
        tiled=True,
    )
    both_halves = lax.all_gather(arrived, "tensor", axis=0, tiled=True).reshape(-1, width_d)
    gate = jnp.dot(both_halves, gate_proj[0], preferred_element_type=jnp.float32)
    upper = jnp.dot(both_halves, up_proj[0], preferred_element_type=jnp.float32)
    hidden = (jax.nn.silu(gate) * upper).astype(jnp.bfloat16)
    down_terms = jnp.dot(hidden, down_proj[0], preferred_element_type=jnp.float32)
    expert_out = lax.psum_scatter(
        down_terms.astype(jnp.bfloat16), "tensor", scatter_dimension=0, tiled=True
    )
    back = lax.all_to_all(
        expert_out.reshape(experts, capacity, width_d),
        "expert",
        split_axis=0,
        concat_axis=0,
        tiled=True,
    )
    picked = back.reshape(-1, width_d)[target]
    mixed = jnp.sum(route_weights[:, :, None] * picked.astype(jnp.float32), axis=1)
    return (attn32 + mixed).astype(jnp.bfloat16)


CHIPS = [(r, b) for r in range(NZ) for b in range(NY)]
NT = (((1,), (1,)), ((), ()))
F32, B16 = jnp.float32, jnp.bfloat16
WHOLE = pl.BlockSpec(memory_space=pltpu.VMEM)
barrier = lax.optimization_barrier


def fold(at):
    return at ^ (at >> 1)


def step_z(z, by):
    return fold((fold(z) + by) % NZ)


def shift_z(value, by=1):
    return lax.ppermute(value, "z", [(z, step_z(z, by)) for z in range(NZ)])


def swap_y(value):
    return lax.ppermute(value, "y", [(0, 1), (1, 0)])


def swap_mate(value):
    return lax.ppermute(value, "z", [(z, z ^ 1) for z in range(NZ)])


def swap_group(value):
    return lax.ppermute(value, "groups", [(0, 1), (1, 0)])


def swap_core(value):
    return lax.ppermute(value, "core", [(0, 1), (1, 0)])


def hand_back(value, r, b):
    if r == 0 and b == 0:
        return value
    pairs = [
        (z * NY + y, step_z(z, -r) * NY + (y ^ b)) for z in range(NZ) for y in range(NY)
    ]
    return lax.ppermute(value, ("z", "y"), pairs)


def call(kernel, outs, scratch, limit, flops, name, *args):
    size = sum(a.size * a.dtype.itemsize for a in args)
    return pl.pallas_call(
        kernel,
        in_specs=[
            pl.BlockSpec(memory_space=pltpu.SMEM) if a.ndim == 1 else WHOLE for a in args
        ],
        out_specs=[WHOLE] * len(outs),
        out_shape=[
            jax.ShapeDtypeStruct(o, B16) if isinstance(o, tuple) else o for o in outs
        ],
        scratch_shapes=scratch,
        compiler_params=pltpu.CompilerParams(vmem_limit_bytes=limit << 20),
        cost_estimate=pl.CostEstimate(flops=flops, bytes_accessed=size, transcendentals=0),
        name=name,
    )(*args)


def prepare(where, kv_latent, routes, route_weights, value_up, experts):
    tok, width = kv_latent.shape
    heads, part, _ = value_up.shape
    half = heads // NC

    def kernel(where, kv, routed, weight, v, out, own, send):
        dense = jnp.zeros((experts, tok), F32)
        number = lax.broadcasted_iota(jnp.int32, (experts, tok), 0)
        for k in range(TOP):
            dense = dense + jnp.where(routed[k : k + 1] == number, weight[k : k + 1], 0.0)
        high = dense.astype(B16)
        low = (dense - high.astype(F32)).astype(B16)
        same = lax.broadcasted_iota(jnp.int32, (tok, tok), 0) == lax.broadcasted_iota(
            jnp.int32, (tok, tok), 1
        )
        eye = jnp.where(same, 1.0, 0.0).astype(B16)
        out[:, :width] = kv[...]
        for n, term in enumerate((high, low)):
            at = width + n * experts
            out[:, at : at + experts] = lax.dot_general(
                eye, term, NT, preferred_element_type=F32
            ).astype(B16)
        for at, ref in ((where[0], own), (1 - where[0], send)):
            ref[...] = v[pl.ds(pl.multiple_of(at * half, half), half)]

    args = (kv_latent, routes.T, route_weights.T, value_up)
    outs = [(tok, width + 2 * experts)] + [(half, part, VD)] * 2
    return pl.pallas_call(
        kernel,
        grid=(1,),
        in_specs=[pl.BlockSpec(memory_space=pltpu.SMEM)]
        + [pl.BlockSpec(a.shape, lambda i, n=a.ndim: (0,) * n) for a in args],
        out_specs=[WHOLE] * len(outs),
        out_shape=[jax.ShapeDtypeStruct(shape, B16) for shape in outs],
        compiler_params=pltpu.CompilerParams(vmem_limit_bytes=60 << 20),
        name="prepare",
    )(where, *args)


def split_heads(where, queries):
    tok, heads, width = queries.shape
    half = heads // NC

    def kernel(where, q, own, send):
        for at, out in ((where[0], own), (1 - where[0], send)):
            first = pl.multiple_of(at * half, half)
            out[...] = jnp.swapaxes(q[:, pl.ds(first, half), :], 0, 1)

    shapes = [(half, tok, width)] * 2
    return call(kernel, shapes, [], 16, 1 << 16, "split_heads", where, queries)


def join_cores(where, own, other):
    heads, part, width = own.shape

    def kernel(where, a, b, out):
        out[:, pl.ds(pl.multiple_of(where[0] * part, part), part), :] = a[...]
        out[:, pl.ds(pl.multiple_of((1 - where[0]) * part, part), part), :] = b[...]

    return call(
        kernel, [(heads, 2 * part, width)], [], 4, 1 << 10, "join_cores", where, own, other
    )[0]


def stack_rows(blocks):
    rows, width = blocks[0].shape

    def kernel(*refs):
        for n, ref in enumerate(refs[:-1]):
            refs[-1][n * rows : (n + 1) * rows] = ref[...]

    return call(kernel, [(rows * len(blocks), width)], [], 2, 1 << 16, "stack_rows", *blocks)[0]


def attend(which, bases, q_own, q_other, k_own, k_other):
    heads, tok, width = q_own.shape
    heads = heads // 2
    half = k_own.shape[0]
    rows = 2 * tok
    hb, sub = 8, 2
    turn = score_scale * 1.4426950408889634

    def kernel(base, qo, qx, ko, kx, out, bias):
        step = lax.broadcasted_iota(jnp.int32, (tok, tok), 0) - lax.broadcasted_iota(
            jnp.int32, (tok, tok), 1
        )
        for d in range(2):
            for n in range(2 * half // tok):
                seen = jnp.where(step + (base[d] - base[2 + n]) >= 0, 0.0, -1e30)
                for j in range(sub):
                    at = j * rows + d * tok
                    bias[at : at + tok, n * tok : (n + 1) * tok] = seen
        own = base[2 + 2 * half // tok]
        first = (own if which == 0 else 1 - own) * heads

        def body(turns, _):
            at = turns * hb
            for g in range(0, hb, sub):
                q = jnp.concatenate(
                    [ref[first + at + j] for j in range(g, g + sub) for ref in (qo, qx)], axis=0
                )
                s0 = lax.dot_general(q, ko[:, :width], NT, preferred_element_type=F32)
                s1 = lax.dot_general(q, kx[:, :width], NT, preferred_element_type=F32)
                s0 = s0 + bias[:, :half]
                s1 = s1 + bias[:, half:]
                top = jnp.maximum(
                    jnp.max(s0, axis=-1, keepdims=True), jnp.max(s1, axis=-1, keepdims=True)
                )
                p0 = jnp.exp2((s0 - top) * turn)
                p1 = jnp.exp2((s1 - top) * turn)
                total = jnp.sum(p0, axis=-1, keepdims=True) + jnp.sum(p1, axis=-1, keepdims=True)
                acc = jnp.dot(p0.astype(B16), ko[:, :LAT], preferred_element_type=F32)
                acc = acc + jnp.dot(p1.astype(B16), kx[:, :LAT], preferred_element_type=F32)
                latent = (acc / total).astype(B16)
                for j in range(sub):
                    out[at + g + j] = latent[j * rows : (j + 1) * rows]
            return 0

        lax.fori_loop(0, heads // hb, body, 0)

    return call(
        kernel,
        [(heads, rows, LAT)],
        [pltpu.VMEM((sub * rows, 2 * half), F32)],
        16,
        2 * heads * rows * 2 * half * (width + LAT),
        "attend",
        bases,
        q_own,
        q_other,
        k_own,
        k_other,
    )[0]


def raise_values(which, where, chips, latent, pieces):
    heads, rows, _ = latent.shape
    part = pieces[0].shape[1]

    def kernel(where, chip, lat, *refs):
        parts, out, lift = refs[:-2], refs[-2], refs[-1]
        first = (where[1] if which == 0 else 1 - where[1]) * heads
        for at, ref in enumerate(parts):
            lift[:, pl.ds(pl.multiple_of(chip[at] * part, part), part), :] = ref[
                pl.ds(first, heads)
            ]
        for j in range(heads):
            out[:, j * VD : (j + 1) * VD] = jnp.dot(
                lat[j], lift[j], preferred_element_type=F32
            ).astype(B16)

    return call(
        kernel,
        [(rows, heads * VD)],
        [pltpu.VMEM((heads, LAT, VD), B16)],
        6,
        2 * heads * rows * LAT * VD,
        "raise_values",
        where,
        chips,
        latent,
        *pieces,
    )[0]


def split_proj(where, flat):
    cols, rows = flat.shape
    half = rows // NC

    def kernel(where, a, own, send):
        own[...] = a[:, pl.ds(pl.multiple_of(where[0] * half, half), half)]
        send[...] = a[:, pl.ds(pl.multiple_of((1 - where[0]) * half, half), half)]

    return call(kernel, [(cols, half)] * 2, [], 4, 1 << 16, "split_proj", where, flat)


def quarter_proj(where, own, other):
    cols, rows = own.shape
    half, part = rows // 2, rows // 8

    def kernel(where, a, b, keep, *sends):
        mine = pl.ds(pl.multiple_of(where[1] * half, half), half)
        start = (1 - where[1]) * half + where[2] * (2 * part)
        for ref, core in ((a, where[0]), (b, 1 - where[0])):
            at = pl.ds(pl.multiple_of(core * cols, 16), cols)
            keep[at, :] = ref[:, mine]
            for n, send in enumerate(sends):
                send[at, :] = ref[:, pl.ds(pl.multiple_of(start + n * part, part), part)]

    return call(
        kernel,
        [(2 * cols, half)] + [(2 * cols, part)] * 2,
        [],
        4,
        1 << 16,
        "quarter_proj",
        where,
        own,
        other,
    )


def join_proj(where, keep, came, across):
    cols, rows = keep.shape
    part = rows // 4

    def kernel(where, a, *refs):
        out = refs[-1]
        out[pl.ds(pl.multiple_of(where[3] * cols, 16), cols), :] = a[...]
        mate = pl.ds(pl.multiple_of((1 - where[3]) * cols, 16), cols)
        for n, ref in enumerate(refs[:-1]):
            group = where[2] if n < 2 else 1 - where[2]
            at = group * (2 * part) + (n % 2) * part
            out[mate, pl.ds(pl.multiple_of(at, part), part)] = ref[...]

    return call(
        kernel, [(2 * cols, rows)], [], 4, 1 << 16, "join_proj", where, keep, *came, *across
    )[0]


def halves(first, second):
    rows = first.shape[0] // 2

    def kernel(a, b, low, high):
        low[...] = a[:rows]
        high[...] = b[rows:]

    return call(kernel, [(rows, first.shape[1])] * 2, [], 2, 1 << 16, "halves", first, second)


def project(columns, *parts):
    rows = sum(part.shape[0] for part in parts)
    cols, depth = columns.shape
    tok = rows // 2

    def kernel(b, *refs):
        keep, send = refs[-2:]
        piece = jnp.concatenate([ref[...] for ref in refs[:-2]], axis=0)
        part = lax.dot_general(piece, b[...], NT, preferred_element_type=F32)
        keep[...] = part[:tok]
        send[...] = part[tok:].astype(B16)

    return call(
        kernel,
        [jax.ShapeDtypeStruct((tok, cols), F32), (tok, cols)],
        [],
        6,
        2 * rows * depth * cols,
        "project",
        columns,
        *parts,
    )


def add(rows, at, *terms):
    def kernel(*refs):
        total = 0.0
        for ref in refs[:-1]:
            block = ref[...] if ref.shape[0] == rows else ref[at : at + rows]
            total = total + block.astype(F32)
        refs[-1][...] = total.astype(B16)

    shape = (rows, terms[0].shape[1])
    return call(kernel, [shape], [], 4, rows * shape[1], "add", *terms)[0]


def sum_strips(kept, mates):
    tok, cols = kept[0].shape
    count = len(kept)

    def kernel(*refs):
        others, outs = refs[count], refs[count + 1 :]
        for n in range(count):
            part = refs[n][...] + others[n * tok : (n + 1) * tok].astype(F32)
            outs[n][...] = part.astype(B16)

    shapes = [(tok, cols)] * count
    return call(kernel, shapes, [], 4, count * tok * cols, "sum_strips", *kept, mates)


def normalise(chips, strips, norm_gain):
    tok, cols = strips[0].shape
    one = cols // 2
    wide = len(CHIPS) * one

    def kernel(chip, gain, *refs):
        parts, attn, normed, stage, full = refs[: len(CHIPS)], *refs[-4:]
        for n, ref in enumerate(parts):
            stage[chip[n]] = ref[...].astype(F32)
        for pair in range(NZ // 2):
            for y in range(NY):
                low = 2 * pair * NY + y
                both = stage[low] + stage[low + NY]
                full[:, low * one : (low + 1) * one] = both[:, :one]
                full[:, (low + NY) * one : (low + NY + 1) * one] = both[:, one:]
        rounded = full[...].astype(B16)
        attn[...] = rounded
        value = rounded.astype(F32)
        scale = lax.rsqrt(jnp.mean(value * value, axis=-1, keepdims=True) + 1e-06)
        normed[...] = (value * scale * gain[...]).astype(B16)

    return call(
        kernel,
        [(tok, wide)] * 2,
        [pltpu.VMEM((len(CHIPS), tok, cols), F32), pltpu.VMEM((tok, wide), F32)],
        10,
        1 << 20,
        "normalise",
        chips,
        norm_gain.reshape(1, -1),
        *strips,
    )


def load(weight):
    def kernel(source, out, sem):
        copy = pltpu.make_async_copy(source, out, sem)
        copy.start()
        copy.wait()

    return pl.pallas_call(
        kernel,
        in_specs=[pl.BlockSpec(memory_space=pltpu.HBM)],
        out_specs=WHOLE,
        out_shape=jax.ShapeDtypeStruct(weight.shape, weight.dtype),
        scratch_shapes=[pltpu.SemaphoreType.DMA],
        compiler_params=pltpu.CompilerParams(vmem_limit_bytes=2 << 20),
        cost_estimate=pl.CostEstimate(flops=0, bytes_accessed=weight.size * 2, transcendentals=0),
        name="load",
    )(weight)


def expert(r, where, k_own, blocks, weights):
    tok, width = blocks[0].shape
    units = weights[0].shape[2]
    fb, nb = 256, 512
    n = len(blocks)
    rows = n * tok
    dense = k_own.shape[1]
    experts = len(CHIPS) * NC

    def kernel(where, ko, *refs):
        mats, refs = refs[: 3 * NC], refs[3 * NC :]
        ins, outs, x, hidden, share = refs[:n], refs[n : 2 * n], *refs[2 * n :]
        lane = lax.broadcasted_iota(jnp.int32, (tok, 2 * experts), 1)
        for b in range(n):
            at = (b * NZ + r) * tok
            table = ko[at : at + tok, dense - 2 * experts :].astype(F32)
            for e in range(NC):
                number = where[4 + e]
                mine = (lane == number) | (lane == number + experts)
                share[b * tok : (b + 1) * tok, e : e + 1] = jnp.sum(
                    jnp.where(mine, table, 0.0), axis=-1, keepdims=True
                )
            x[b * tok : (b + 1) * tok] = ins[b][...]
        for e in range(NC):
            gate_w, up_w = mats[3 * e], mats[3 * e + 1]
            for f in range(0, units, fb):
                gate = jnp.dot(x[...], gate_w[0, :, f : f + fb], preferred_element_type=F32)
                upper = jnp.dot(x[...], up_w[0, :, f : f + fb], preferred_element_type=F32)
                hidden[e, :, f : f + fb] = (jax.nn.silu(gate) * upper).astype(B16)
        for c in range(0, width, nb):
            out = 0.0
            for e in range(NC):
                down = jnp.dot(
                    hidden[e], mats[3 * e + 2][0, :, c : c + nb], preferred_element_type=F32
                )
                out = out + down * share[:, e : e + 1]
            out = out.astype(B16)
            for b in range(n):
                outs[b][:, c : c + nb] = out[b * tok : (b + 1) * tok]

    return call(
        kernel,
        [(tok, width)] * n,
        [
            pltpu.VMEM((rows, width), B16),
            pltpu.VMEM((NC, rows, units), B16),
            pltpu.VMEM((rows, NC), F32),
        ],
        6,
        12 * rows * width * units,
        "expert",
        where,
        k_own,
        *weights,
        *blocks,
    )


def boxed(
    queries,
    kv_latent,
    value_up,
    out_proj,
    norm_gain,
    gate_proj,
    up_proj,
    down_proj,
    routes,
    route_weights,
):
    tok, heads, width = queries.shape
    group, z, y, core = (lax.axis_index(name) for name in ("groups", "z", "y", "core"))
    experts = NZ * NY * NC
    place = (z * NY + y) * NC + core
    kind = fold(z) % 2
    where = jnp.stack([core, kind, group, z % 2, place, place ^ 1]).astype(jnp.int32)
    up_chips = jnp.stack([step_z(z, r) * NY + (y ^ b) for r, b in CHIPS])
    down_chips = jnp.stack([step_z(z, -r) * NY + (y ^ b) for r, b in CHIPS])
    key_chips = jnp.stack([step_z(z, -r) * NY + (y ^ b) for b in range(NY) for r in range(NZ)])
    bases = [jnp.stack([place, place ^ 1]), key_chips * NC + core, key_chips * NC + (core ^ 1)]
    bases = jnp.concatenate([jnp.concatenate(bases) * tok, kind[None]]).astype(jnp.int32)
    where, up_chips, down_chips, bases, kv_latent = barrier(
        (where, up_chips, down_chips, bases, kv_latent)
    )

    pack, lift_own, lift_send = prepare(
        where, kv_latent, routes, route_weights, value_up, experts
    )
    queries, out_proj, pack = barrier((queries, out_proj, pack))
    keys = [pack] + [shift_z(pack, r) for r in range(1, NZ)]
    lift = join_cores(where, lift_own, swap_core(lift_send))
    queries, out_proj, lift = barrier((queries, out_proj, lift))
    up1, side0 = shift_z(lift), swap_y(lift)
    proj_own, proj_send = split_proj(where, out_proj.T)
    q_own, q_send = split_heads(where, queries)
    *keys, up1, side0, q_own, q_send, proj_own, proj_send = barrier(
        (*keys, up1, side0, q_own, q_send, proj_own, proj_send)
    )

    column = stack_rows(keys)
    beside = swap_y(column)
    up2 = shift_z(up1)
    q_other, proj_other = swap_core(q_send), swap_core(proj_send)
    beside, up2, up1, side0, q_other, proj_other = barrier(
        (beside, up2, up1, side0, q_other, proj_other)
    )

    k_own = stack_rows([column, beside])
    k_other = swap_core(k_own)
    up3, side1 = shift_z(up2), swap_y(up1)
    near = attend(0, bases, q_own, q_other, k_own, k_other)
    up3, side1, up2, near, q_own, proj_own, proj_other = barrier(
        (up3, side1, up2, near, q_own, proj_own, proj_other)
    )

    keep, send0, send1 = quarter_proj(where, proj_own, proj_other)
    send0, send1, q_own = barrier((send0, send1, q_own))
    side2, side3, came0 = swap_y(up2), swap_y(up3), swap_mate(send0)
    far = attend(1, bases, q_own, q_other, k_own, k_other)
    side2, side3, came0, far = barrier((side2, side3, came0, far))
    lifts = (lift, side0, up1, side1, up2, side2, up3, side3)
    near = raise_values(0, where, down_chips, near, lifts)

    near, far, send1, came0, gate_proj = barrier((near, far, send1, came0, gate_proj))
    row2, side0 = shift_z(near, 2), swap_y(near)
    far = raise_values(1, where, down_chips, far, lifts)
    high = swap_y(halves(far, far)[1])
    came1, across0 = swap_mate(send1), swap_group(came0)
    gate_other = swap_core(gate_proj)
    row2, side0, high, came1, across0, gate_other = barrier(
        (row2, side0, high, came1, across0, gate_other)
    )
    row1, side2, across1 = shift_z(far), swap_y(row2), swap_group(came1)
    row1, side2, across1, up_proj = barrier((row1, side2, across1, up_proj))
    up_other = swap_core(up_proj)
    row3, side1 = shift_z(far, -1), swap_y(row1)
    columns = join_proj(where, keep, (came0, came1), (across0, across1))
    parts = {(0, 0): project(columns, near)}
    for chip, piece in (((0, 1), side0), ((2, 0), row2), ((2, 1), side2), ((1, 0), row1)):
        parts[chip] = project(columns, piece)
    early = list(parts)
    row3, side1, *done = barrier((row3, side1, *(x for chip in early for x in parts[chip])))
    parts = {chip: done[2 * n : 2 * n + 2] for n, chip in enumerate(early)}
    low = halves(row3, row3)[0]
    low, high, row3, side1 = barrier((low, high, row3, side1))
    low, high = swap_y(low), shift_z(high, -1)
    parts[1, 1], parts[3, 0] = project(columns, side1), project(columns, row3)
    low, high, up_other, *done = barrier((low, high, up_other, *parts[1, 1], *parts[3, 0]))
    parts[1, 1], parts[3, 0] = done[:2], done[2:]
    parts[3, 1] = project(columns, low, high)
    mates = swap_core(stack_rows([parts[chip][1] for chip in CHIPS]))
    down_proj, mates = barrier((down_proj, mates))
    down_other = swap_core(down_proj)
    sums = sum_strips([parts[chip][0] for chip in CHIPS], mates)
    strips = {chip: hand_back(total, *chip) for chip, total in zip(CHIPS, sums)}
    attn, normed = normalise(up_chips, [strips[chip] for chip in CHIPS], norm_gain)

    gate_proj, up_proj, down_proj, normed = barrier((gate_proj, up_proj, down_proj, normed))
    row1, side0 = shift_z(normed), swap_y(normed)
    weights = [load(w) for w in (gate_proj, up_proj, down_proj)]
    weights += [gate_other, up_other, down_other]
    row1, side0, *weights = barrier((row1, side0, *weights))

    def run(r, *blocks):
        return expert(r, where, k_own, blocks, weights)

    row2, side1 = shift_z(row1), swap_y(row1)
    near0, far0 = run(0, normed, side0)
    row2, side1, near0, far0 = barrier((row2, side1, near0, far0))
    row3, side2 = shift_z(row2), swap_y(row2)
    near1, far1 = run(1, row1, side1)
    row3, side2, near1, far1 = barrier((row3, side2, near1, far1))
    side3, side1 = shift_z(side2), swap_y(far1)
    near2, far2 = run(2, row2, side2)
    side3, side1, near2, far2 = barrier((side3, side1, near2, far2))
    acc, side2 = shift_z(add(tok, 0, near1, side1)), swap_y(far2)
    near3, far3 = run(3, row3, side3)
    acc, side2, near3, far3 = barrier((acc, side2, near3, far3))
    acc, side3 = shift_z(add(tok, 0, acc, near2, side2)), swap_y(far3)
    acc, side3, far0 = barrier((acc, side3, far0))
    acc, side0 = shift_z(add(tok, 0, acc, near3, side3)), swap_y(far0)
    return add(tok, 0, attn, acc, near0, side0)


def solution(mesh):
    names = ("expert",)
    body = local
    shape = mesh.shape
    if shape["expert"] == NZ * NY * NC and shape["tensor"] == 1 and shape["groups"] == 2:
        mesh = Mesh(mesh.devices.reshape(2, NZ, NY, NC, 1), ("groups", "z", "y", "core", "tensor"))
        names = ("z", "y", "core")
        body = boxed
    every = ("groups",) + names
    in_specs = (
        P(every, "tensor", None),
        P(every, None),
        P("tensor", names, None),
        P("tensor", names),
        P(),
        P(names, None, "tensor"),
        P(names, None, "tensor"),
        P(names, "tensor", None),
        P(every + ("tensor",), None),
        P(every + ("tensor",), None),
    )
    out_specs = P(every + ("tensor",), None)
    return jax.shard_map(body, mesh=mesh, in_specs=in_specs, out_specs=out_specs, check_vma=False)
```
